128 devices in a mesh: section: 4 (over x_lo, core), fsdp: 32 (over x_hi, z, y).
Axes of the slice: x: 4 (x_hi: 2, x_lo: 2; x = x_hi * 2 + x_lo), y: 4, z: 4, core: 2. Of those that a mesh axis runs over, the one named last changes fastest.
Arguments:
- saved_inputs: bfloat16 [4, 2, 32, 512, 1536], P('section', None, 'fsdp'), may hold values from -6 to 6
- grad_outputs: bfloat16 [2, 32, 512, 1536], P(None, 'fsdp'), may hold values from -6 to 6
- lengths: int32 [2, 32], P(None, 'fsdp'), may hold values from 256 to 512, as said below
- pointwise: bfloat16 [4, 1536, 1536], P('section', 'fsdp'), may hold values from -0.15625 to 0.15625
- depth_kernel: bfloat16 [4, 5, 1536], P('section', None, 'fsdp'), may hold values from -2.5 to 2.5
- norm_gain: bfloat16 [4, 1536], P('section', 'fsdp'), may hold values from 0.5 to 1.5
Outputs:
- frame_grads: bfloat16 [4, 2, 32, 512, 1536], P('section', None, 'fsdp')
- pointwise_grad: float32 [4, 1536, 1536], P('section', 'fsdp')
- kernel_grad: float32 [4, 5, 1536], P('section', None, 'fsdp')
- gain_grad: float32 [4, 1536], P('section', 'fsdp')
The draws below stay inside these ranges and needn't reach their ends.
Inputs may be any that keep to these rules, and one draw needn't show every extreme that they name: `lengths`: frames at and after an utterance's length are padding; some utterance fills all 512 slots.
All inputs are finite; a program needn't handle non-finite values.
Results may differ from the reference program's by a relative error of at most 0.0057.
Values may be sent and summed in bfloat16 or wider, within the bound.
No kernel may reach another device: no remote copies, remote signals or barrier semaphores. Data moves between devices by JAX's collectives and lax.ppermute only.
A program may use at most 128 MiB of HBM per device.

```python
import jax
import jax.numpy as jnp
from jax import lax

D = 1536
KERNEL = 5
FRAMES = 512
MICRO = 2
SECTIONS = 4
BATCH = 32
TOKENS = 32768


def draw_lengths(key, part):
    values = jax.random.randint(key, (MICRO * BATCH,), FRAMES // 2, FRAMES + 1)
    chosen = jax.random.randint(jax.random.fold_in(key, 7), (), 0, MICRO * BATCH)
    filled = jnp.where(jnp.arange(MICRO * BATCH) == chosen, FRAMES, values)
    return filled.reshape(MICRO, BATCH).astype(jnp.int32)


def steps_of(rng, dims, split, least, high):
    factor_of = 1.0
    for position, shards_of in split:
        heights = jax.random.uniform(jax.random.fold_in(jax.random.fold_in(rng, 6), position), (shards_of,), jnp.float32, least / len(split), high / len(split))
        factor_of = factor_of * jnp.repeat(jnp.exp(heights), dims[position] // shards_of).reshape((-1,) + (1,) * (len(dims) - 1 - position))
    return factor_of


def gaussian(key, extent, deviation, limit, cuts=(), held_as=jnp.bfloat16):
    entries = deviation * jax.random.normal(key, extent, jnp.float32)
    if cuts:
        entries = entries * steps_of(key, extent, cuts, -0.22, 0.18)
    return jnp.clip(entries, -limit, limit).astype(held_as)


def setup_inputs(seed: int = 0) -> dict:
    splits = jax.random.split(jax.random.key(seed), 7)
    saved_inputs = gaussian(splits[0], (SECTIONS, MICRO, BATCH, FRAMES, D), 1.0, 6.0, ((0, 4), (2, 32)))
    grad_outputs = gaussian(splits[1], (MICRO, BATCH, FRAMES, D), 1.0, 6.0, ((1, 32),))
    lengths = draw_lengths(jax.random.fold_in(splits[6], 71), 0)
    pointwise = gaussian(splits[3], (SECTIONS, D, D), D ** -0.5, 0.15625, ((0, 4), (1, 32)))
    depth_kernel = gaussian(splits[4], (SECTIONS, KERNEL, D), KERNEL ** -0.5, 2.5, ((0, 4), (2, 32)))
    norm_gain = jnp.clip(0.5 + 1.0 * jax.random.uniform(splits[5], (SECTIONS, D), jnp.float32) ** steps_of(splits[5], (SECTIONS, D), ((0, 4), (1, 32)), -0.2, 0.2), 0.5, 1.5).astype(jnp.bfloat16)
    return dict(saved_inputs=saved_inputs, grad_outputs=grad_outputs, lengths=lengths, pointwise=pointwise, depth_kernel=depth_kernel, norm_gain=norm_gain)


EPSILON = 1e-05

def depthwise(signal, kernel):
    tap_count = kernel.shape[0]
    margin = (tap_count - 1) // 2
    length = signal.shape[-2]
    widths = [(0, 0)] * (signal.ndim - 2) + [(margin, margin), (0, 0)]
    padded = jnp.pad(signal, widths)
    running = jnp.zeros(signal.shape, jnp.float32)
    for offset in range(tap_count):
        running = running + kernel[offset].astype(jnp.float32) * padded[..., offset:offset + length, :]
    return running

def tap_sums(upstream, signal, tap_count):
    margin = (tap_count - 1) // 2
    length = signal.shape[-2]
    widths = [(0, 0)] * (signal.ndim - 2) + [(margin, margin), (0, 0)]
    padded = jnp.pad(signal, widths)
    leading = tuple(range(signal.ndim - 1))
    return jnp.stack([lax.optimization_barrier(jnp.sum(upstream * padded[..., offset:offset + length, :], axis=leading)) for offset in range(tap_count)])

def activation(inputs, present, kernel, gains):
    hidden = inputs.astype(jnp.float32) * present
    mixed = depthwise(hidden, kernel)
    average = lax.optimization_barrier(jnp.mean(mixed, axis=-1, keepdims=True))
    centred = mixed - average
    inverse = lax.rsqrt(lax.optimization_barrier(jnp.mean(centred * centred, axis=-1, keepdims=True)) + EPSILON)
    normed = centred * inverse
    gained = normed * gains.astype(jnp.float32)
    logistic = jax.nn.sigmoid(gained)
    return (hidden, inverse, normed, gained, logistic)

def through_norm(grad_activated, hidden, inverse, normed, gained, logistic, kernel, gains, upstream, present):
    grad_gained = grad_activated * (logistic + gained * logistic * (1.0 - logistic))
    leading = tuple(range(grad_gained.ndim - 1))
    gain_term = lax.optimization_barrier(jnp.sum(grad_gained * normed, axis=leading))
    grad_normed = grad_gained * gains.astype(jnp.float32)
    grad_mixed = inverse * (grad_normed - lax.optimization_barrier(jnp.mean(grad_normed, axis=-1, keepdims=True)) - normed * lax.optimization_barrier(jnp.mean(grad_normed * normed, axis=-1, keepdims=True)))
    kernel_term = tap_sums(grad_mixed, hidden, kernel.shape[0])
    grad_hidden = depthwise(grad_mixed, kernel[::-1])
    grad_inputs = (upstream + grad_hidden * present).astype(jnp.bfloat16)
    return (grad_inputs, kernel_term, gain_term)

def reference(saved_inputs, grad_outputs, lengths, pointwise, depth_kernel, norm_gain):
    factor = float(TOKENS) ** (-0.5)
    places = jnp.arange(FRAMES, dtype=jnp.int32)
    point_sums = [jnp.zeros((D, D), jnp.float32) for section_num in range(SECTIONS)]
    kernel_sums = [jnp.zeros((KERNEL, D), jnp.float32) for section_num in range(SECTIONS)]
    gain_sums = [jnp.zeros((D,), jnp.float32) for section_num in range(SECTIONS)]
    frame_rows = [[None] * MICRO for section_num in range(SECTIONS)]
    for micro_id in range(MICRO):
        present = (places[None, :] < lengths[micro_id][:, None]).astype(jnp.float32)[..., None]
        upstream = grad_outputs[micro_id].astype(jnp.float32)
        for section_num in range(SECTIONS - 1, -1, -1):
            kernel = depth_kernel[section_num]
            gains = norm_gain[section_num]
            projection = pointwise[section_num].astype(jnp.float32)
            hidden, inverse, normed, gained, logistic = activation(saved_inputs[section_num, micro_id], present, kernel, gains)
            activated = (gained * logistic).astype(jnp.bfloat16)
            grad_masked = (upstream * present).astype(jnp.bfloat16)
            activ_flat = activated.reshape(-1, D).astype(jnp.float32)
            masked_flat = grad_masked.reshape(-1, D).astype(jnp.float32)
            point_sums[section_num] = point_sums[section_num] + jnp.dot(activ_flat.T, masked_flat, precision=lax.Precision.HIGHEST)
            grad_activated = jnp.dot(masked_flat, projection.T, precision=lax.Precision.HIGHEST).reshape(grad_masked.shape)
            grad_inputs, kernel_term, gain_term = through_norm(grad_activated, hidden, inverse, normed, gained, logistic, kernel, gains, upstream, present)
            kernel_sums[section_num] = kernel_sums[section_num] + kernel_term
            gain_sums[section_num] = gain_sums[section_num] + gain_term
            frame_rows[section_num][micro_id] = grad_inputs
            upstream = grad_inputs.astype(jnp.float32)
    frame_grads = jnp.stack([jnp.stack(frame_rows[section_num]) for section_num in range(SECTIONS)])
    pointwise_grad = jnp.stack(point_sums) * factor
    kernel_grad = jnp.stack(kernel_sums) * factor
    gain_grad = jnp.stack(gain_sums) * factor
    return (frame_grads, pointwise_grad, kernel_grad, gain_grad)
```

```python
import functools

import jax
import jax.numpy as jnp
import numpy as np
from jax import lax
from jax.experimental import pallas as pl
from jax.experimental.pallas import tpu as pltpu
from jax.sharding import Mesh
from jax.sharding import PartitionSpec as P

EPSILON = 1e-05
F32 = jnp.float32
BF16 = jnp.bfloat16
LANES = 128
PAD = 8
ANY = pl.BlockSpec(memory_space=pl.ANY)
SMEM = pl.BlockSpec(memory_space=pltpu.SMEM)
VMEM = pl.BlockSpec(memory_space=pltpu.VMEM)

GATHERED = [(0, 0), (0, 1), (3, 0), (3, 1), (1, 0), (1, 1), (2, 0), (2, 1)]
SCATTERED = [(2, 0), (1, 1), (2, 1), (3, 0), (1, 0), (3, 1), (0, 0), (0, 1)]


def params(limit, **kw):
    return pltpu.CompilerParams(vmem_limit_bytes=limit << 20, **kw)


def cost(us):
    return pl.CostEstimate(flops=int(us * 1.0e9), bytes_accessed=1 << 20, transcendentals=0)


def tables():
    gather = np.zeros((2, 4, 4, 2, 5, 8), np.int32)
    scatter = np.zeros((2, 4, 4, 2, 32), np.int32)
    for x in range(2):
        for z in range(4):
            for y in range(4):
                for half in range(2):
                    inner, outer = (y, z) if half == 0 else (z, y)

                    def block(o, i, r):
                        a, b, c = (outer + o) % 4, (inner + i) % 4, (x + r) % 2
                        zz, yy = (a, b) if half == 0 else (b, a)
                        return c * 16 + zz * 4 + yy

                    for slot, o in enumerate((0, 3, 1, 2)):
                        for j, (i, r) in enumerate(GATHERED):
                            gather[x, z, y, half, slot, j] = block(o, i, r)
                    for o in range(4):
                        for j, (i, r) in enumerate(SCATTERED):
                            base = {2: (0, 8), 1: (16, 4), 3: (12, 20), 0: (24, 28)}[o]
                            place = base[0] + j if j < 4 else base[1] + j - 4
                            scatter[x, z, y, half, block(o, i, r)] = place
    return gather.reshape(2, 4, 4, -1), scatter.reshape(2, 4, 4, -1)


def forward_kernel(lens, x_ref, taps, normed_ref, slope_ref, inv_ref, act_ref, hid, mix):
    m = pl.program_id(0)
    length = lens[m]
    frames, feats = x_ref.shape[1:]
    cols = feats // LANES
    for c in range(cols):
        hid[c, 0:PAD, :] = jnp.zeros((PAD, LANES), F32)
        hid[c, PAD + frames : 2 * PAD + frames, :] = jnp.zeros((PAD, LANES), F32)

    def load(i, carry):
        r = pl.multiple_of(i * 16, 16)
        rows = r + lax.broadcasted_iota(jnp.int32, (16, LANES), 0)
        keep = rows < length
        for c in range(cols):
            v = x_ref[0, pl.ds(r, 16), c * LANES : (c + 1) * LANES].astype(F32)
            hid[c, pl.ds(r + PAD, 16), :] = jnp.where(keep, v, 0.0)
        return carry

    lax.fori_loop(0, frames // 16, load, 0)
    for c in range(cols):
        span = slice(c * LANES, (c + 1) * LANES)
        weights = [jnp.broadcast_to(taps[k : k + 1, span], (64, LANES)) for k in range(5)]

        def conv(i, carry):
            r = pl.multiple_of(i * 64, 64)
            total = weights[0] * hid[c, pl.ds(r + PAD - 2, 64), :]
            for k in range(1, 5):
                total = total + weights[k] * hid[c, pl.ds(r + PAD - 2 + k, 64), :]
            mix[pl.ds(r, 64), span] = total
            return carry

        lax.fori_loop(0, frames // 64, conv, 0)

    def norm(i, carry):
        r = pl.multiple_of(i * 16, 16)
        mixed = mix[pl.ds(r, 16), :]
        centred = mixed - jnp.mean(mixed, axis=-1, keepdims=True)
        inverse = lax.rsqrt(jnp.mean(centred * centred, axis=-1, keepdims=True) + EPSILON)
        gain = taps[5:6, :]
        normed = centred * inverse
        gained = normed * gain
        logistic = jax.nn.sigmoid(gained)
        normed_ref[0, pl.ds(r, 16), :] = normed.astype(BF16)
        slope_ref[0, pl.ds(r, 16), :] = (
            (logistic + gained * logistic * (1.0 - logistic)) * gain
        ).astype(BF16)
        act_ref[0, pl.ds(r, 16), :] = (gained * logistic).astype(BF16)
        inv_ref[0, pl.ds(r, 16), :] = jnp.broadcast_to(inverse, (16, LANES))
        return carry

    lax.fori_loop(0, frames // 16, norm, 0, unroll=2)


def forward(lens, x, taps):
    micro, frames, feats = x.shape
    block = pl.BlockSpec((1, frames, feats), lambda m: (m, 0, 0))
    return pl.pallas_call(
        forward_kernel,
        grid=(micro,),
        in_specs=[SMEM, block, pl.BlockSpec(taps.shape, lambda m: (0, 0))],
        out_specs=[block, block, pl.BlockSpec((1, frames, LANES), lambda m: (m, 0, 0)), block],
        out_shape=[
            jax.ShapeDtypeStruct(x.shape, BF16),
            jax.ShapeDtypeStruct(x.shape, BF16),
            jax.ShapeDtypeStruct((micro, frames, LANES), F32),
            jax.ShapeDtypeStruct(x.shape, BF16),
        ],
        scratch_shapes=[
            pltpu.VMEM((feats // LANES, frames + 2 * PAD, LANES), F32),
            pltpu.VMEM((frames, feats), F32),
        ],
        compiler_params=params(40),
        cost_estimate=cost(12),
    )(lens, x, taps)


def relay_kernel(first, step, grads, come, *rest):
    (wa, wb), rest = (rest[:5], rest[5:10]), rest[10:]
    normed_in, slope_in, inv_in, taps, rest = *rest[:4], rest[4:]
    if not first:
        rest = rest[4:]
    send, frame_out, masked_out, mixed_out, gain_out = rest[:5]
    w, up, gm, normed, slope, inv, ga, gmix, out, gsum, sems = rest[5:]
    frames, feats = up.shape
    cols = feats // LANES
    half = feats // 2
    rows = 48
    active, slot, last, length = step[0], step[1], step[2], step[3]

    def pieces():
        made = []
        for h, parts in enumerate((wa, wb)):
            for p in range(5):
                for j in range(parts[p].shape[0]):
                    at = h * 40 + (p * 8 + j if p < 4 else 28 + j)
                    place = pl.multiple_of(step[8 + at] * rows, 16)
                    made.append(
                        pltpu.make_async_copy(
                            parts[p].at[j],
                            w.at[pl.ds(place, rows), pl.ds(h * half, half)],
                            sems.at[0],
                        )
                    )
        return made

    @pl.when(active == 1)
    def _():
        @pl.when(last == 1)
        def _():
            pltpu.make_async_copy(grads.at[slot], up, sems.at[1]).start()

        @pl.when(last == 0)
        def _():
            pltpu.make_async_copy(come, up, sems.at[1]).start()

        weights = pieces()
        for copy in weights:
            copy.start()
        others = [
            pltpu.make_async_copy(normed_in.at[slot], normed, sems.at[2]),
            pltpu.make_async_copy(slope_in.at[slot], slope, sems.at[3]),
            pltpu.make_async_copy(inv_in.at[slot], inv, sems.at[4]),
        ]
        for copy in others:
            copy.start()
        for c in range(cols):
            gmix[c, 0:PAD, :] = jnp.zeros((PAD, LANES), F32)
            gmix[c, PAD + frames : 2 * PAD + frames, :] = jnp.zeros((PAD, LANES), F32)
        pltpu.make_async_copy(come, up, sems.at[1]).wait()

        def mask(i, carry):
            r = pl.multiple_of(i * 16, 16)
            keep = r + lax.broadcasted_iota(jnp.int32, (16, feats), 0) < length
            v = up[pl.ds(r, 16), :].astype(F32)
            gm[pl.ds(r, 16), :] = jnp.where(keep, v, 0.0).astype(BF16)
            return carry

        lax.fori_loop(0, frames // 16, mask, 0)
        masked_copy = pltpu.make_async_copy(gm, masked_out.at[slot], sems.at[5])
        masked_copy.start()
        for copy in weights:
            copy.wait()

        def multiply(n, carry):
            r = pl.multiple_of(n * 256, 256)
            ga[:, pl.ds(r, 256)] = lax.dot_general(
                gm[...], w[pl.ds(r, 256), :], (((1,), (1,)), ((), ())), preferred_element_type=F32
            )
            return carry

        lax.fori_loop(0, feats // 256, multiply, 0)
        for copy in others:
            copy.wait()
        gsum[...] = jnp.zeros_like(gsum)

        def through(i, carry):
            r = pl.multiple_of(i * 16, 16)
            gn = ga[pl.ds(r, 16), :] * slope[pl.ds(r, 16), :].astype(F32)
            nm = normed[pl.ds(r, 16), :].astype(F32)
            both = gn * nm
            gsum[...] += both[:8] + both[8:]
            a = jnp.sum(gn, axis=-1, keepdims=True) * (1.0 / feats)
            b = jnp.sum(both, axis=-1, keepdims=True) * (1.0 / feats)
            mixed = inv[pl.ds(r, 16), 0:1] * (gn - a - nm * b)
            for c in range(cols):
                gmix[c, pl.ds(r + PAD, 16), :] = mixed[:, c * LANES : (c + 1) * LANES]
            return carry

        lax.fori_loop(0, frames // 16, through, 0, unroll=2)
        saved = [
            pltpu.make_async_copy(gmix, mixed_out.at[slot], sems.at[6]),
            pltpu.make_async_copy(gsum, gain_out.at[slot], sems.at[7]),
        ]
        for copy in saved:
            copy.start()
        for c in range(cols):
            span = slice(c * LANES, (c + 1) * LANES)
            kernel = [jnp.broadcast_to(taps[k : k + 1, span], (64, LANES)) for k in range(5)]

            def conv(i, carry):
                r = pl.multiple_of(i * 64, 64)
                total = kernel[4] * gmix[c, pl.ds(r + PAD - 2, 64), :]
                for k in range(1, 5):
                    total = total + kernel[4 - k] * gmix[c, pl.ds(r + PAD - 2 + k, 64), :]
                keep = r + lax.broadcasted_iota(jnp.int32, (64, LANES), 0) < length
                result = up[pl.ds(r, 64), span].astype(F32) + jnp.where(keep, total, 0.0)
                out[pl.ds(r, 64), span] = result.astype(BF16)
                return carry

            lax.fori_loop(0, frames // 64, conv, 0)
        ends = [
            pltpu.make_async_copy(out, send, sems.at[8]),
            pltpu.make_async_copy(out, frame_out.at[slot], sems.at[9]),
        ]
        for copy in ends:
            copy.start()
        for copy in [masked_copy] + saved + ends:
            copy.wait()


def relay(step, grads, come, weights, saved, taps, state):
    micro, frames, feats = grads.shape
    cols = feats // LANES
    first = state is None
    shapes = [
        jax.ShapeDtypeStruct((frames, feats), BF16),
        jax.ShapeDtypeStruct((micro, frames, feats), BF16),
        jax.ShapeDtypeStruct((micro, frames, feats), BF16),
        jax.ShapeDtypeStruct((micro, cols, frames + 2 * PAD, LANES), F32),
        jax.ShapeDtypeStruct((micro, 8, feats), F32),
    ]
    operands = [step, grads, come, *weights, *saved, taps]
    specs = [SMEM] + [ANY] * (len(operands) - 2) + [VMEM]
    aliases = {}
    if not first:
        aliases = {len(operands) + i: 1 + i for i in range(4)}
        operands += list(state)
        specs += [ANY] * 4
    out = pl.pallas_call(
        functools.partial(relay_kernel, first),
        in_specs=specs,
        out_specs=[ANY] * 5,
        out_shape=shapes,
        input_output_aliases=aliases,
        scratch_shapes=[
            pltpu.VMEM((feats, feats), BF16),
            pltpu.VMEM((frames, feats), BF16),
            pltpu.VMEM((frames, feats), BF16),
            pltpu.VMEM((frames, feats), BF16),
            pltpu.VMEM((frames, feats), BF16),
            pltpu.VMEM((frames, LANES), F32),
            pltpu.VMEM((frames, feats), F32),
            pltpu.VMEM((cols, frames + 2 * PAD, LANES), F32),
            pltpu.VMEM((frames, feats), BF16),
            pltpu.VMEM((8, feats), F32),
            pltpu.SemaphoreType.DMA((10,)),
        ],
        compiler_params=params(40),
        cost_estimate=cost(8),
    )(*operands)
    return out[0], tuple(out[1:])


def weight_kernel(step, act_in, masked_in, come, *rest):
    outs, (act, gm, acc, block, sems) = rest[:6], rest[6:]
    frames = come.shape[0]
    feats = come.shape[1]
    half = feats // 2
    head, length = step[0], step[1]
    copies = [
        pltpu.make_async_copy(act_in.at[0], act.at[pl.ds(0, frames)], sems.at[0]),
        pltpu.make_async_copy(act_in.at[1], act.at[pl.ds(frames, frames)], sems.at[1]),
        pltpu.make_async_copy(masked_in.at[0], gm.at[pl.ds(0, frames)], sems.at[2]),
    ]
    for copy in copies:
        copy.start()

    @pl.when(head == 1)
    def _():
        pltpu.make_async_copy(come, gm.at[pl.ds(frames, frames)], sems.at[3]).start()

    @pl.when(head == 0)
    def _():
        pltpu.make_async_copy(masked_in.at[1], gm.at[pl.ds(frames, frames)], sems.at[3]).start()

    pltpu.make_async_copy(come, gm.at[pl.ds(frames, frames)], sems.at[3]).wait()

    def mask(i, carry):
        r = pl.multiple_of(i * 16, 16)
        keep = r + lax.broadcasted_iota(jnp.int32, (16, feats), 0) < length
        v = gm[pl.ds(r + frames, 16), :].astype(F32)
        gm[pl.ds(r + frames, 16), :] = jnp.where(keep, v, 0.0).astype(BF16)
        return carry

    lax.fori_loop(0, frames // 16, mask, 0)
    for copy in copies:
        copy.wait()
    leaving = []
    for h in range(2):

        def multiply(n, carry):
            r = pl.multiple_of(n * 256, 256)
            acc[pl.ds(r, 256), :] = lax.dot_general(
                act[:, pl.ds(r, 256)],
                gm[:, h * half : (h + 1) * half],
                (((0,), (0,)), ((), ())),
                preferred_element_type=F32,
            )
            return carry

        lax.fori_loop(0, feats // 256, multiply, 0)

        def place(b, carry):
            r = pl.multiple_of(b * 48, 16)
            block[h, step[8 + h * 32 + b]] = acc[pl.ds(r, 48), :].astype(BF16)
            return carry

        lax.fori_loop(0, 32, place, 0)
        for p, (start, size) in enumerate(((0, 8), (8, 8), (16, 16))):
            copy = pltpu.make_async_copy(
                block.at[h, pl.ds(start, size)], outs[h * 3 + p], sems.at[4 + h * 3 + p]
            )
            copy.start()
            leaving.append(copy)
    for copy in leaving:
        copy.wait()


def weight_terms(step, act, masked, come):
    frames, feats = come.shape
    half = feats // 2
    sizes = (8, 8, 16)
    return pl.pallas_call(
        weight_kernel,
        in_specs=[SMEM, ANY, ANY, ANY],
        out_specs=[ANY] * 6,
        out_shape=[jax.ShapeDtypeStruct((n, 48, half), BF16) for n in sizes] * 2,
        scratch_shapes=[
            pltpu.VMEM((2 * frames, feats), BF16),
            pltpu.VMEM((2 * frames, feats), BF16),
            pltpu.VMEM((feats, half), F32),
            pltpu.VMEM((2, 32, 48, half), BF16),
            pltpu.SemaphoreType.DMA((10,)),
        ],
        compiler_params=params(40),
        cost_estimate=cost(8),
    )(step, act, masked, come)


def tap_kernel(lens, x_ref, mixed_ref, gain_ref, taps, out, hid):
    m = pl.program_id(0)
    length = lens[m]
    frames, feats = x_ref.shape[1:]
    cols = feats // LANES

    @pl.when(m == 0)
    def _():
        out[...] = jnp.zeros_like(out)

    for c in range(cols):
        hid[c, 0:PAD, :] = jnp.zeros((PAD, LANES), F32)
        hid[c, PAD + frames : 2 * PAD + frames, :] = jnp.zeros((PAD, LANES), F32)

    def load(i, carry):
        r = pl.multiple_of(i * 16, 16)
        keep = r + lax.broadcasted_iota(jnp.int32, (16, LANES), 0) < length
        for c in range(cols):
            v = x_ref[0, pl.ds(r, 16), c * LANES : (c + 1) * LANES].astype(F32)
            hid[c, pl.ds(r + PAD, 16), :] = jnp.where(keep, v, 0.0)
        return carry

    lax.fori_loop(0, frames // 16, load, 0)
    for c in range(cols):
        span = slice(c * LANES, (c + 1) * LANES)

        def add(i, sums):
            r = pl.multiple_of(i * 32, 32)
            grown = list(sums)
            for q in range(4):
                g = mixed_ref[0, c, pl.ds(r + PAD + 8 * q, 8), :]
                for k in range(5):
                    grown[k] = grown[k] + g * hid[c, pl.ds(r + PAD - 2 + k + 8 * q, 8), :]
            return tuple(grown)

        sums = lax.fori_loop(0, frames // 32, add, (jnp.zeros((8, LANES), F32),) * 5)
        for k in range(5):
            out[k : k + 1, span] += jnp.sum(sums[k], axis=0, keepdims=True)
    out[5:6, :] += jnp.sum(gain_ref[0], axis=0, keepdims=True) / taps[5:6, :]


def tap_terms(lens, x, mixed, gain, taps):
    micro, frames, feats = x.shape
    return pl.pallas_call(
        tap_kernel,
        grid=(micro,),
        in_specs=[
            SMEM,
            pl.BlockSpec((1, frames, feats), lambda m: (m, 0, 0)),
            pl.BlockSpec((1,) + mixed.shape[1:], lambda m: (m, 0, 0, 0)),
            pl.BlockSpec((1, 8, feats), lambda m: (m, 0, 0)),
            pl.BlockSpec(taps.shape, lambda m: (0, 0)),
        ],
        out_specs=pl.BlockSpec((8, feats), lambda m: (0, 0)),
        out_shape=jax.ShapeDtypeStruct((8, feats), F32),
        scratch_shapes=[pltpu.VMEM((feats // LANES, frames + 2 * PAD, LANES), F32)],
        compiler_params=params(40),
        cost_estimate=cost(8),
    )(lens, x, mixed, gain, taps)


def shift(x, axis, d):
    n = lax.axis_size(axis)
    return lax.ppermute(x, axis, [(i, (i + d) % n) for i in range(n)])


def swap(x, axis, d):
    n = lax.axis_size(axis)
    return lax.ppermute(x, axis, [(i, i ^ d) for i in range(n)])


def gather_weights(shard):
    half = shard.shape[1] // 2
    other = swap(shard, "xh", 1)
    pairs = [
        jnp.stack([shard[:, :half], other[:, :half]]),
        jnp.stack([shard[:, half:], other[:, half:]]),
    ]

    def ring(own, axis):
        cut = own.shape[0] // 2
        left, right = shift(own, axis, 1), shift(own, axis, -1)
        return own, left, right, shift(left[:cut], axis, 1), shift(right[cut:], axis, -1)

    first = [jnp.concatenate(ring(p, a)) for p, a in zip(pairs, ("y", "z"))]
    return [ring(p, a) for p, a in zip(first, ("z", "y"))]


def sum_everywhere(x):
    for axis, d in (("xh", 1), ("z", 1), ("z", 2), ("y", 1), ("y", 2)):
        x = x + swap(x, axis, d)
    return x


def scatter_ring(plus, minus, kept, axis):
    n = plus.shape[0] // 2
    up_a, dn_b, own_a, own_b = (kept[i * n : (i + 1) * n].astype(F32) for i in range(4))
    p, q = shift(plus, axis, 1), shift(minus, axis, -1)
    far_p = shift((up_a + p[:n].astype(F32)).astype(BF16), axis, 1)
    far_q = shift((dn_b + q[:n].astype(F32)).astype(BF16), axis, -1)
    a = own_a + far_p.astype(F32) + q[n:].astype(F32)
    b = own_b + far_q.astype(F32) + p[n:].astype(F32)
    return a, b


def scatter_weights(parts):
    first = [scatter_ring(*parts[:3], "z"), scatter_ring(*parts[3:], "y")]
    second = []
    for (a, b), axis in zip(first, ("y", "z")):
        a, b = a.astype(BF16), b.astype(BF16)
        second.append(scatter_ring(a[:2], a[2:], b, axis))
    own = jnp.concatenate([a[0] for a, _ in second], axis=1)
    give = jnp.concatenate([b[0] for _, b in second], axis=1).astype(BF16)
    return own + swap(give, "xh", 1).astype(F32)


def body(saved_inputs, grad_outputs, lengths, pointwise, depth_kernel, norm_gain):
    section = lax.axis_index("section")
    x, z, y = (lax.axis_index(a) for a in ("xh", "z", "y"))
    inputs = saved_inputs[0, :, 0]
    grads = grad_outputs[:, 0]
    lens = lengths[:, 0]
    micro, frames, features = inputs.shape
    factor = float(32 * micro * frames) ** (-0.5)
    place = (x * 16 + z * 4 + y) * 48

    small = jnp.concatenate([depth_kernel[0], norm_gain[0:1]], axis=0)
    small = lax.dynamic_update_slice(jnp.zeros((6, features), BF16), small, (0, place))
    taps = jnp.pad(sum_everywhere(small).astype(F32), ((0, 2), (0, 0)))
    halves = gather_weights(pointwise[0])
    weights = [*halves[0], *halves[1]]
    normed, slope, inverse, act = forward(lens, inputs, taps)

    gather_table, scatter_table = tables()
    gather_at = jnp.asarray(gather_table)[x, z, y]
    scatter_at = jnp.asarray(scatter_table)[x, z, y]

    def turn(state, come, who):
        slot = jnp.asarray(who, jnp.int32)[section]
        at = jnp.maximum(slot, 0)
        flags = [slot >= 0, at, section == 3, lens[at], 0, 0, 0, 0]
        step = jnp.concatenate([jnp.stack([jnp.asarray(f, jnp.int32) for f in flags]), gather_at])
        return relay(step, grads, come, weights, (normed, slope, inverse), taps, state)

    def hop(block, route):
        return lax.ppermute(block, "section", route)

    sent, state = turn(None, grads[0], (-1, -1, -1, 0))
    come = hop(sent, [(3, 2)])
    sent, state = turn(state, come, (-1, -1, 0, 1))
    come = hop(sent, [(3, 2), (2, 1), (1, 0)])
    sent, state = turn(state, come, (-1, 0, 1, -1))
    come = hop(sent, [(3, 2), (2, 1), (1, 0)])
    sent, state = turn(state, come, (0, 1, -1, -1))
    come = hop(sent, [(1, 0)])
    head = section == 0
    flags = [head, lens[1], 0, 0, 0, 0, 0, 0]
    step = jnp.concatenate([jnp.stack([jnp.asarray(f, jnp.int32) for f in flags]), scatter_at])
    parts = weight_terms(step, act, state[1], come)
    point_share = scatter_weights(parts)
    sent, state = turn(state, come, (1, -1, -1, -1))
    frame_out, _, mixed, gain = state
    terms = sum_everywhere(tap_terms(lens, inputs, mixed, gain, taps))
    share = lax.dynamic_slice(terms, (0, place), (8, 48)) * factor
    return (
        frame_out[None, :, None],
        (point_share * factor)[None],
        share[None, :5],
        share[5:6],
    )


def solution(mesh):
    fine = Mesh(mesh.devices.reshape(4, 2, 4, 4), ("section", "xh", "z", "y"))
    fsdp = ("xh", "z", "y")
    return jax.shard_map(
        body,
        mesh=fine,
        in_specs=(
            P("section", None, fsdp, None, None),
            P(None, fsdp, None, None),
            P(None, fsdp),
            P("section", fsdp, None),
            P("section", None, fsdp),
            P("section", fsdp),
        ),
        out_specs=(
            P("section", None, fsdp, None, None),
            P("section", fsdp, None),
            P("section", None, fsdp),
            P("section", fsdp),
        ),
        check_vma=False,
    )
```

```python
import functools

import jax
import jax.numpy as jnp
import numpy as np
from jax import lax
from jax.experimental import pallas as pl
from jax.experimental.pallas import tpu as pltpu
from jax.sharding import Mesh
from jax.sharding import PartitionSpec as P

EPSILON = 1e-05
F32 = jnp.float32
BF16 = jnp.bfloat16
LANES = 128
PAD = 8
ANY = pl.BlockSpec(memory_space=pl.ANY)
HBM = pl.BlockSpec(memory_space=pltpu.HBM)
SMEM = pl.BlockSpec(memory_space=pltpu.SMEM)
VMEM = pl.BlockSpec(memory_space=pltpu.VMEM)

GATHERED = [(0, 0), (0, 1), (3, 0), (3, 1), (1, 0), (1, 1), (2, 0), (2, 1)]
SCATTERED = [(2, 0), (1, 1), (2, 1), (3, 0), (1, 0), (3, 1), (0, 0), (0, 1)]


def params(limit, **kw):
    return pltpu.CompilerParams(vmem_limit_bytes=limit << 20, **kw)


def cost(us):
    return pl.CostEstimate(flops=int(us * 1.0e9), bytes_accessed=1 << 20, transcendentals=0)


def tables():
    gather = np.zeros((2, 4, 4, 2, 5, 8), np.int32)
    scatter = np.zeros((2, 4, 4, 2, 32), np.int32)
    for x in range(2):
        for z in range(4):
            for y in range(4):
                for half in range(2):
                    inner, outer = (y, z) if half == 0 else (z, y)

                    def block(o, i, r):
                        a, b, c = (outer + o) % 4, (inner + i) % 4, (x + r) % 2
                        zz, yy = (a, b) if half == 0 else (b, a)
                        return c * 16 + zz * 4 + yy

                    for slot, o in enumerate((0, 3, 1, 2)):
                        for j, (i, r) in enumerate(GATHERED):
                            gather[x, z, y, half, slot, j] = block(o, i, r)
                    for o in range(4):
                        for j, (i, r) in enumerate(SCATTERED):
                            base = {2: (0, 8), 1: (16, 4), 3: (12, 20), 0: (24, 28)}[o]
                            place = base[0] + j if j < 4 else base[1] + j - 4
                            scatter[x, z, y, half, block(o, i, r)] = place
    return gather.reshape(2, 4, 4, -1), scatter.reshape(2, 4, 4, -1)


def forward_kernel(m, lens, x_in, taps, normed_ref, slope_ref, inv_ref, act_ref, x_ref, hid, mix, act, sem):
    length = lens[m]
    frames, feats = x_ref.shape
    cols = feats // LANES
    copy = pltpu.make_async_copy(x_in.at[m], x_ref, sem)
    copy.start()
    for c in range(cols):
        hid[c, 0:PAD, :] = jnp.zeros((PAD, LANES), F32)
        hid[c, PAD + frames : 2 * PAD + frames, :] = jnp.zeros((PAD, LANES), F32)
    copy.wait()

    def load(i, carry):
        r = pl.multiple_of(i * 16, 16)
        rows = r + lax.broadcasted_iota(jnp.int32, (16, LANES), 0)
        keep = rows < length
        for c in range(cols):
            v = x_ref[pl.ds(r, 16), c * LANES : (c + 1) * LANES].astype(F32)
            hid[c, pl.ds(r + PAD, 16), :] = jnp.where(keep, v, 0.0)
        return carry

    lax.fori_loop(0, frames // 16, load, 0, unroll=2)

    def conv(i, carry):
        r = pl.multiple_of(i * 64, 64)
        for c in range(cols):
            span = slice(c * LANES, (c + 1) * LANES)
            total = taps[0:1, span] * hid[c, pl.ds(r + PAD - 2, 64), :]
            for k in range(1, 5):
                total = total + taps[k : k + 1, span] * hid[c, pl.ds(r + PAD - 2 + k, 64), :]
            mix[pl.ds(r, 64), span] = total
        return carry

    lax.fori_loop(0, frames // 64, conv, 0)

    def norm(i, carry):
        r = pl.multiple_of(i * 16, 16)
        keep = r + lax.broadcasted_iota(jnp.int32, (16, 1), 0) < length
        mixed = mix[pl.ds(r, 16), :]
        centred = mixed - jnp.mean(mixed, axis=-1, keepdims=True)
        inverse = lax.rsqrt(jnp.mean(centred * centred, axis=-1, keepdims=True) + EPSILON)
        gain = taps[5:6, :]
        normed = centred * inverse
        gained = normed * gain
        logistic = jax.nn.sigmoid(gained)
        normed_ref[pl.ds(r, 16), :] = normed.astype(BF16)
        slope_ref[pl.ds(r, 16), :] = (
            (logistic + gained * logistic * (1.0 - logistic)) * gain
        ).astype(BF16)
        act[pl.ds(r, 16), :] = jnp.where(keep, gained * logistic, 0.0).astype(BF16)
        inv_ref[pl.ds(r, 16), :] = jnp.broadcast_to(inverse, (16, LANES))
        return carry

    lax.fori_loop(0, frames // 16, norm, 0, unroll=2)

    for c in range(feats // 256):
        act_ref[c * 256 : (c + 1) * 256, :] = act[:, c * 256 : (c + 1) * 256].T


def forward(m, lens, x, taps):
    micro, frames, feats = x.shape
    return pl.pallas_call(
        functools.partial(forward_kernel, m),
        in_specs=[SMEM, HBM, VMEM],
        out_specs=[VMEM] * 4,
        out_shape=[
            jax.ShapeDtypeStruct((frames, feats), BF16),
            jax.ShapeDtypeStruct((frames, feats), BF16),
            jax.ShapeDtypeStruct((frames, LANES), F32),
            jax.ShapeDtypeStruct((feats, frames), BF16),
        ],
        scratch_shapes=[
            pltpu.VMEM((frames, feats), BF16),
            pltpu.VMEM((feats // LANES, frames + 2 * PAD, LANES), F32),
            pltpu.VMEM((frames, feats), F32),
            pltpu.VMEM((frames, feats), BF16),
            pltpu.SemaphoreType.DMA,
        ],
        compiler_params=params(60),
        cost_estimate=cost(8),
    )(lens, x, taps)


def relay_kernel(first, who, meta, grads, come, come_one, *rest):
    (wa, wb), rest = (rest[:5], rest[5:10]), rest[10:]
    (normed_in, slope_in, inv_in), taps, rest = (rest[0:2], rest[2:4], rest[4:6]), rest[6], rest[7:]
    if not first:
        rest = rest[2:]
    send, mixed_out, gain_out = rest[:3]
    w, up, normed, slope, inv, ga, gmix, narrow, out, gsum, sems = rest[3:]
    frames, feats = up.shape
    cols = feats // LANES
    half = feats // 2
    rows = 48
    head = 288
    section = meta[0]
    turn = sum(jnp.where(section == i, m, 0) for i, m in enumerate(who))
    active, slot = turn >= 0, jnp.maximum(turn, 0)
    last, length = section == 3, meta[1 + slot]

    def pieces():
        made = []
        for h, parts in enumerate((wa, wb)):
            for p in range(5):
                for j in range(parts[p].shape[0]):
                    at = h * 40 + (p * 8 + j if p < 4 else 28 + j)
                    place = pl.multiple_of(meta[8 + at] * rows, 16)
                    made.append(
                        pltpu.make_async_copy(
                            parts[p].at[j],
                            w.at[pl.ds(place, rows), pl.ds(h * half, half)],
                            sems.at[0],
                        )
                    )
        return made

    def fetch(source):
        pltpu.make_async_copy(source.at[pl.ds(0, head)], up.at[pl.ds(0, head)], sems.at[1]).start()
        pltpu.make_async_copy(
            source.at[pl.ds(head, frames - head)], up.at[pl.ds(head, frames - head)], sems.at[8]
        ).start()

    @pl.when(active)
    def _():
        @pl.when(last)
        def _():
            fetch(grads.at[slot])

        @pl.when(section == 1)
        def _():
            fetch(come_one)

        @pl.when(jnp.logical_and(section != 3, section != 1))
        def _():
            fetch(come)

        weights = pieces()
        for copy in weights:
            copy.start()
        for m in range(2):

            @pl.when(slot == m)
            def _():
                pltpu.make_async_copy(normed_in[m], normed, sems.at[2]).start()
                pltpu.make_async_copy(slope_in[m], slope, sems.at[3]).start()
                pltpu.make_async_copy(inv_in[m], inv, sems.at[4]).start()

        for c in range(cols):
            gmix[c, 0:PAD, :] = jnp.zeros((PAD, LANES), F32)
            gmix[c, PAD + frames : 2 * PAD + frames, :] = jnp.zeros((PAD, LANES), F32)
        gsum[...] = jnp.zeros_like(gsum)

        def multiply(start, size, n):
            r = pl.multiple_of(n * 256, 256)
            ga[start : start + size, pl.ds(r, 256)] = lax.dot_general(
                up[start : start + size, :],
                w[pl.ds(r, 256), :],
                (((1,), (1,)), ((), ())),
                preferred_element_type=F32,
            )

        def through(i):
            r = pl.multiple_of(i * 16, 16)
            keep = r + lax.broadcasted_iota(jnp.int32, (16, 1), 0) < length
            gn = ga[pl.ds(r, 16), :] * slope[pl.ds(r, 16), :].astype(F32)
            gn = jnp.where(keep, gn, 0.0)
            nm = normed[pl.ds(r, 16), :].astype(F32)
            both = gn * nm
            gsum[...] += both[:8] + both[8:]
            a = jnp.sum(gn, axis=-1, keepdims=True) * (1.0 / feats)
            b = jnp.sum(both, axis=-1, keepdims=True) * (1.0 / feats)
            mixed = inv[pl.ds(r, 16), 0:1] * (gn - a - nm * b)
            narrow[pl.ds(r, 16), :] = mixed.astype(BF16)
            for c in range(cols):
                gmix[c, pl.ds(r + PAD, 16), :] = mixed[:, c * LANES : (c + 1) * LANES]

        def first_part(n, carry):
            multiply(0, head, n)
            return carry

        def second_part(n, carry):
            multiply(head, frames - head, n)
            for q in range(3):
                through(n * 3 + q)
            return carry

        def third_part(n, carry):
            for q in range(2):
                through(head // 16 + n * 2 + q)
            return carry

        pltpu.make_async_copy(come.at[pl.ds(0, head)], up.at[pl.ds(0, head)], sems.at[1]).wait()
        for copy in weights:
            copy.wait()
        lax.fori_loop(0, feats // 256, first_part, 0)
        pltpu.make_async_copy(
            come.at[pl.ds(head, frames - head)], up.at[pl.ds(head, frames - head)], sems.at[8]
        ).wait()
        pltpu.make_async_copy(normed_in[0], normed, sems.at[2]).wait()
        pltpu.make_async_copy(slope_in[0], slope, sems.at[3]).wait()
        pltpu.make_async_copy(inv_in[0], inv, sems.at[4]).wait()
        lax.fori_loop(0, feats // 256, second_part, 0)
        upper, lower = pl.ds(0, head), pl.ds(head, frames - head)
        early = pltpu.make_async_copy(narrow.at[upper], mixed_out.at[slot, upper], sems.at[9])
        early.start()
        lax.fori_loop(0, (frames - head) // 32, third_part, 0)
        saved = [
            pltpu.make_async_copy(narrow.at[lower], mixed_out.at[slot, lower], sems.at[5]),
            pltpu.make_async_copy(gsum, gain_out.at[slot], sems.at[6]),
        ]
        for copy in saved:
            copy.start()

        def conv(i, carry):
            r = pl.multiple_of(i * 64, 64)
            keep = r + lax.broadcasted_iota(jnp.int32, (64, LANES), 0) < length
            for c in range(cols):
                span = slice(c * LANES, (c + 1) * LANES)
                total = taps[4:5, span] * gmix[c, pl.ds(r + PAD - 2, 64), :]
                for k in range(1, 5):
                    total = total + taps[4 - k : 5 - k, span] * gmix[c, pl.ds(r + PAD - 2 + k, 64), :]
                result = up[pl.ds(r, 64), span].astype(F32) + jnp.where(keep, total, 0.0)
                out[pl.ds(r, 64), span] = result.astype(BF16)
            part = pl.ds(r, 64)
            pltpu.make_async_copy(out.at[part], send.at[part], sems.at[7]).start()
            return carry

        lax.fori_loop(0, frames // 64, conv, 0)
        pltpu.make_async_copy(out, send, sems.at[7]).wait()
        for copy in [early] + saved:
            copy.wait()


def relay(who, meta, grads, come, come_one, weights, saved, taps, state):
    micro, frames, feats = grads.shape
    cols = feats // LANES
    first = state is None
    shapes = [
        jax.ShapeDtypeStruct((frames, feats), BF16),
        jax.ShapeDtypeStruct((micro, frames, feats), BF16),
        jax.ShapeDtypeStruct((micro, 8, feats), F32),
    ]
    operands = [meta, grads, come, come_one, *weights, *saved, taps]
    specs = [SMEM, HBM, ANY, ANY] + [HBM] * (len(operands) - 5) + [VMEM]
    aliases = {}
    if not first:
        aliases = {len(operands) + i: 1 + i for i in range(2)}
        operands += list(state)
        specs += [HBM] * 2
    out = pl.pallas_call(
        functools.partial(relay_kernel, first, who),
        in_specs=specs,
        out_specs=[ANY] + [HBM] * 2,
        out_shape=shapes,
        input_output_aliases=aliases,
        scratch_shapes=[
            pltpu.VMEM((feats, feats), BF16),
            pltpu.VMEM((frames, feats), BF16),
            pltpu.VMEM((frames, feats), BF16),
            pltpu.VMEM((frames, feats), BF16),
            pltpu.VMEM((frames, LANES), F32),
            pltpu.VMEM((frames, feats), F32),
            pltpu.VMEM((cols, frames + 2 * PAD, LANES), F32),
            pltpu.VMEM((frames, feats), BF16),
            pltpu.VMEM((frames, feats), BF16),
            pltpu.VMEM((8, feats), F32),
            pltpu.SemaphoreType.DMA((10,)),
        ],
        compiler_params=params(60),
        cost_estimate=cost(1),
    )(*operands)
    return out[0], tuple(out[1:])


def weight_kernel(meta, act_a, act_b, *rest):
    sources, outs, (act, gm, acc, block, sems) = rest[:7], rest[7:13], rest[13:]
    feats, frames = act_a.shape
    half = feats // 2
    section = meta[0]
    copies = [
        pltpu.make_async_copy(act_a, act.at[:, pl.ds(0, frames)], sems.at[0]),
        pltpu.make_async_copy(act_b, act.at[:, pl.ds(frames, frames)], sems.at[1]),
    ]
    for copy in copies:
        copy.start()
    for m in range(2):
        for owner in range(4):

            @pl.when(section == owner)
            def _():
                source = sources[0].at[m] if owner == 3 else sources[1 + 2 * owner + m]
                place = gm.at[pl.ds(m * frames, frames)]
                pltpu.make_async_copy(source, place, sems.at[2 + m]).start()

    for m in range(2):
        copies[m].wait()
        pltpu.make_async_copy(sources[1], gm.at[pl.ds(m * frames, frames)], sems.at[2 + m]).wait()
    leaving = []
    for h in range(2):

        def multiply(n, carry):
            r = pl.multiple_of(n * 256, 256)
            acc[pl.ds(r, 256), :] = lax.dot_general(
                act[pl.ds(r, 256), :],
                gm[:, h * half : (h + 1) * half],
                (((1,), (0,)), ((), ())),
                preferred_element_type=F32,
            )
            return carry

        lax.fori_loop(0, feats // 256, multiply, 0)

        def place(b, carry):
            r = pl.multiple_of(b * 48, 16)
            block[h, meta[88 + h * 32 + b]] = acc[pl.ds(r, 48), :].astype(BF16)
            return carry

        lax.fori_loop(0, 32, place, 0, unroll=4)
        for p, (start, size) in enumerate(((0, 8), (8, 8), (16, 16))):
            copy = pltpu.make_async_copy(
                block.at[h, pl.ds(start, size)], outs[h * 3 + p], sems.at[4 + h * 3 + p]
            )
            copy.start()
            leaving.append(copy)
    for copy in leaving:
        copy.wait()


def weight_terms(meta, acts, grads, comes):
    feats, frames = acts[0].shape
    half = feats // 2
    sizes = (8, 8, 16)
    operands = [meta, *acts, grads, *comes]
    return pl.pallas_call(
        weight_kernel,
        in_specs=[SMEM, ANY, ANY, HBM] + [ANY] * len(comes),
        out_specs=[ANY] * 6,
        out_shape=[jax.ShapeDtypeStruct((n, 48, half), BF16) for n in sizes] * 2,
        scratch_shapes=[
            pltpu.VMEM((feats, 2 * frames), BF16),
            pltpu.VMEM((2 * frames, feats), BF16),
            pltpu.VMEM((feats, half), F32),
            pltpu.VMEM((2, 32, 48, half), BF16),
            pltpu.SemaphoreType.DMA((10,)),
        ],
        compiler_params=params(60),
        cost_estimate=cost(8),
    )(*operands)


def tap_kernel(meta, x_ref, mixed_ref, gain_ref, taps, *rest):
    sent, (out, frame_out, hid, held, sems) = rest[:6], rest[6:]
    m = pl.program_id(0)
    section = meta[0]
    length = meta[1 + m]
    frames, feats = x_ref.shape[1:]
    cols = feats // LANES

    @pl.when(m == 0)
    def _():
        out[...] = jnp.zeros_like(out)
        for owner, turns in enumerate(((4, 5), (3, 4), (1, 2), (0, 1))):

            @pl.when(section == owner)
            def _():
                for p in range(2):
                    pltpu.make_async_copy(sent[turns[p]], held.at[p], sems.at[p]).start()

    for c in range(cols):
        hid[c, 0:PAD, :] = jnp.zeros((PAD, LANES), F32)
        hid[c, PAD + frames : 2 * PAD + frames, :] = jnp.zeros((PAD, LANES), F32)

    def load(i, carry):
        r = pl.multiple_of(i * 16, 16)
        keep = r + lax.broadcasted_iota(jnp.int32, (16, LANES), 0) < length
        for c in range(cols):
            v = x_ref[0, pl.ds(r, 16), c * LANES : (c + 1) * LANES].astype(F32)
            hid[c, pl.ds(r + PAD, 16), :] = jnp.where(keep, v, 0.0)
        return carry

    lax.fori_loop(0, frames // 16, load, 0, unroll=2)
    for c in range(cols):
        span = slice(c * LANES, (c + 1) * LANES)

        def add(i, sums):
            r = pl.multiple_of(i * 32, 32)
            grown = list(sums)
            wide = mixed_ref[0, pl.ds(r, 32), span].astype(F32)
            for q in range(4):
                g = wide[8 * q : 8 * q + 8]
                for k in range(5):
                    grown[k] = grown[k] + g * hid[c, pl.ds(r + PAD - 2 + k + 8 * q, 8), :]
            return tuple(grown)

        sums = lax.fori_loop(0, frames // 32, add, (jnp.zeros((8, LANES), F32),) * 5)
        for k in range(5):
            out[k : k + 1, span] += jnp.sum(sums[k], axis=0, keepdims=True)
    out[5:6, :] += jnp.sum(gain_ref[0], axis=0, keepdims=True) / taps[5:6, :]
    leave = pltpu.make_async_copy(held, frame_out, sems.at[2])

    @pl.when(m == 0)
    def _():
        for p in range(2):
            pltpu.make_async_copy(sent[0], held.at[p], sems.at[p]).wait()
        leave.start()

    @pl.when(m == 1)
    def _():
        leave.wait()


def tap_terms(meta, x, mixed, gain, taps, sent):
    micro, frames, feats = x.shape
    return pl.pallas_call(
        tap_kernel,
        grid=(micro,),
        in_specs=[
            SMEM,
            pl.BlockSpec((1, frames, feats), lambda m: (m, 0, 0)),
            pl.BlockSpec((1, frames, feats), lambda m: (m, 0, 0)),
            pl.BlockSpec((1, 8, feats), lambda m: (m, 0, 0)),
            pl.BlockSpec(taps.shape, lambda m: (0, 0)),
        ]
        + [HBM] * 6,
        out_specs=[pl.BlockSpec((8, feats), lambda m: (0, 0)), HBM],
        out_shape=[
            jax.ShapeDtypeStruct((8, feats), F32),
            jax.ShapeDtypeStruct(x.shape, BF16),
        ],
        scratch_shapes=[
            pltpu.VMEM((feats // LANES, frames + 2 * PAD, LANES), F32),
            pltpu.VMEM(x.shape, BF16),
            pltpu.SemaphoreType.DMA((3,)),
        ],
        compiler_params=params(60),
        cost_estimate=cost(6),
    )(meta, x, mixed, gain, taps, *sent)


def shift(x, axis, d):
    n = lax.axis_size(axis)
    return lax.ppermute(x, axis, [(i, (i + d) % n) for i in range(n)])


def swap(x, axis, d):
    n = lax.axis_size(axis)
    return lax.ppermute(x, axis, [(i, i ^ d) for i in range(n)])


def gather_weights(shard, small):
    rows, width = shard.shape
    half = width // 2
    extra = jnp.zeros((16, half), BF16).at[0, : small.size].set(small.reshape(-1))
    own = [jnp.concatenate([shard[:, :half], extra]), shard[:, half:]]
    pairs = [jnp.stack([p, swap(p, "xh", 1)]) for p in own]

    def near(p, axis):
        return [p] + [shift(p, axis, d) for d in (1, -1, 2)]

    first = [jnp.concatenate(near(p, a)) for p, a in zip(pairs, ("y", "z"))]
    packed = first[0][:, rows, : small.size]
    packed = jnp.stack(near(packed, "z"))
    packed = packed.reshape(4, 4, 2, *small.shape)
    packed = jnp.stack([packed[i] for i in (0, 2, 3, 1)])
    packed = jnp.stack([packed[:, i] for i in (0, 2, 3, 1)], axis=1)
    x, z, y = (lax.axis_index(a) for a in ("xh", "z", "y"))
    packed = jnp.tile(packed, (2, 2, 2, 1, 1))
    zero = jnp.zeros((), jnp.int32)
    packed = lax.dynamic_slice(
        packed, ((4 - z) % 4, (4 - y) % 4, (2 - x) % 2, zero, zero), (4, 4, 2, *small.shape)
    )
    whole = packed.transpose(3, 2, 0, 1, 4).reshape(small.shape[0], width)

    def ring(own, axis):
        cut = own.shape[0] // 2
        left, right = shift(own, axis, 1), shift(own, axis, -1)
        return own, left, right, shift(left[:cut], axis, 1), shift(right[cut:], axis, -1)

    pieces = [ring(p[:, :rows], a) for p, a in zip(first, ("z", "y"))]
    return [*pieces[0], *pieces[1]], whole


def scatter_near(pieces, axis):
    total = pieces[0]
    for d in (1, 2, 3):
        total = total + shift(pieces[d].astype(BF16), axis, d).astype(F32)
    return total


def scatter_weights(parts, terms):
    rings = (parts[:3], "z"), (parts[3:], "y")
    moved = [(shift(p[0], a, 1), shift(p[1], a, -1)) for p, a in rings]
    moved, terms = lax.optimization_barrier((moved, terms))
    halves = []
    for (parts_, axis), (p, q) in zip(rings, moved):
        kept = parts_[2]
        n = kept.shape[0] // 4
        up_a, dn_b, own_a, own_b = (kept[i * n : (i + 1) * n].astype(F32) for i in range(4))
        far_p = shift((up_a + p[:n].astype(F32)).astype(BF16), axis, 1)
        far_q = shift((dn_b + q[:n].astype(F32)).astype(BF16), axis, -1)
        a = own_a + far_p.astype(F32) + q[n:].astype(F32)
        b = own_b + far_q.astype(F32) + p[n:].astype(F32)
        halves.append(jnp.concatenate([a, b]))
    a, b = halves
    packed = scatter_near(terms, "z")
    extra = jnp.zeros((8, 16, a.shape[2]), F32).at[:, 0, : packed.shape[1]].set(packed)
    a = jnp.concatenate([a, extra], axis=1)
    own = []
    for blocks, axis in ((a, "y"), (b, "z")):
        pieces = [
            jnp.stack([blocks[SCATTERED.index((i, r))] for r in range(2)]) for i in range(4)
        ]
        summed = scatter_near(pieces, axis)
        own.append(summed[0] + swap(summed[1].astype(BF16), "xh", 1).astype(F32))
    rows = own[1].shape[0]
    return jnp.concatenate([own[0][:rows], own[1]], axis=1), own[0][rows, : packed.shape[1]]


def body(saved_inputs, grad_outputs, lengths, pointwise, depth_kernel, norm_gain):
    section = lax.axis_index("section")
    x, z, y = (lax.axis_index(a) for a in ("xh", "z", "y"))
    inputs = saved_inputs[0, :, 0]
    grads = grad_outputs[:, 0]
    lens = lengths[:, 0]
    micro, frames, features = inputs.shape
    factor = float(32 * micro * frames) ** (-0.5)

    gather_table, scatter_table = tables()
    table = jnp.asarray(np.concatenate([gather_table, scatter_table], axis=-1).reshape(32, -1))
    table = lax.dynamic_index_in_dim(table, x * 16 + z * 4 + y, 0, keepdims=False)
    meta = jnp.concatenate([section[None], lens, jnp.zeros((5,), jnp.int32), table])

    small = jnp.concatenate([depth_kernel[0], norm_gain[0:1]], axis=0)
    weights, small = gather_weights(pointwise[0], small)
    taps = jnp.pad(small.astype(F32), ((0, 2), (0, 0)))
    made = [forward(m, lens, inputs, taps) for m in range(2)]
    saved = [made[m][i] for i in range(3) for m in range(2)]
    acts = [made[m][3] for m in range(2)]

    def turn(state, come, come_one, who):
        return relay(who, meta, grads, come, come_one, weights, saved, taps, state)

    def hop(block, source):
        return lax.ppermute(block, "section", [(source, source - 1)])

    outs = [None] * 6
    outs[0], state = turn(None, saved[0], saved[0], (-1, -1, -1, 0))
    two_0 = hop(outs[0], 3)
    outs[1], state = turn(state, two_0, two_0, (-1, -1, 0, 1))
    two_1, one_0 = hop(outs[1], 3), hop(outs[1], 2)
    outs[2], state = turn(state, two_1, two_1, (-1, -1, 1, -1))
    one_1 = hop(outs[2], 2)
    outs[3], state = turn(state, one_0, one_0, (-1, 0, -1, -1))
    outs[3], one_1 = lax.optimization_barrier((outs[3], one_1))
    zero_0 = hop(outs[3], 1)
    outs[4], state = turn(state, zero_0, one_1, (0, 1, -1, -1))
    zero_1 = hop(outs[4], 1)
    parts = weight_terms(meta, acts, grads, [zero_0, zero_1, one_0, one_1, two_0, two_1])
    outs[5], (mixed, gain) = turn(state, zero_1, zero_1, (1, -1, -1, -1))
    sums, frame_out = tap_terms(meta, inputs, mixed, gain, taps, outs)

    def terms():
        blocks = (sums[:6] * factor).reshape(6, 2, 4, 4, 48)
        blocks = blocks.transpose(2, 3, 1, 0, 4).reshape(4, 4, 2, 288)
        blocks = lax.dynamic_slice(
            jnp.tile(blocks, (2, 2, 2, 1)), (z, y, x, jnp.zeros((), jnp.int32)), (4, 4, 2, 288)
        )
        return jnp.stack([blocks[:, i, r] for i, r in SCATTERED], axis=1)

    point_share, share = scatter_weights(parts, terms())
    share = share.reshape(6, 48)
    return (
        frame_out[None, :, None],
        (point_share * factor)[None],
        share[None, :5],
        share[5:6],
    )


def solution(mesh):
    fine = Mesh(mesh.devices.reshape(4, 2, 4, 4), ("section", "xh", "z", "y"))
    fsdp = ("xh", "z", "y")
    return jax.shard_map(
        body,
        mesh=fine,
        in_specs=(
            P("section", None, fsdp, None, None),
            P(None, fsdp, None, None),
            P(None, fsdp),
            P("section", fsdp, None),
            P("section", None, fsdp),
            P("section", fsdp),
        ),
        out_specs=(
            P("section", None, fsdp, None, None),
            P("section", fsdp, None),
            P("section", None, fsdp),
            P("section", fsdp),
        ),
        check_vma=False,
    )
```

```python
import functools

import jax
import jax.numpy as jnp
import numpy as np
from jax import lax
from jax.experimental import pallas as pl
from jax.experimental.pallas import tpu as pltpu
from jax.sharding import Mesh
from jax.sharding import PartitionSpec as P

EPSILON = 1e-05
F32 = jnp.float32
BF16 = jnp.bfloat16
LANES = 128
PAD = 8
ANY = pl.BlockSpec(memory_space=pl.ANY)
HBM = pl.BlockSpec(memory_space=pltpu.HBM)
SMEM = pl.BlockSpec(memory_space=pltpu.SMEM)
VMEM = pl.BlockSpec(memory_space=pltpu.VMEM)

GATHERED = [(0, 0), (0, 1), (3, 0), (3, 1), (1, 0), (1, 1), (2, 0), (2, 1)]
SCATTERED = [(i, r) for i in range(4) for r in range(2)]


def params(limit, **kw):
    return pltpu.CompilerParams(vmem_limit_bytes=limit << 20, **kw)


def cost(us):
    return pl.CostEstimate(flops=int(us * 1.0e9), bytes_accessed=1 << 20, transcendentals=0)


def tables():
    gather = np.zeros((2, 2, 4, 4, 2, 4, 8), np.int32)
    scatter = np.zeros((2, 2, 4, 4, 2, 32), np.int32)
    for core, x, z, y, half in np.ndindex(2, 2, 4, 4, 2):
        inner, outer = (y, z) if half == 0 else (z, y)

        def block(o, i, r):
            a, b, c = (outer + o) % 4, (inner + i) % 4, (x + r) % 2
            zz, yy = (a, b) if half == 0 else (b, a)
            return c * 16 + zz * 4 + yy

        for slot, o in enumerate((0, 3, 1, 2)):
            for j, (i, r) in enumerate(GATHERED):
                gather[core, x, z, y, half, slot, j] = block(o, i, r)
        base = {2: 0, 3: 8, 1: 16, 0: 24} if core == 0 else {2: 8, 1: 0, 3: 16, 0: 24}
        for o in range(4):
            for j, (i, r) in enumerate(SCATTERED):
                scatter[core, x, z, y, half, block(o, i, r)] = base[o] + j
    return np.concatenate([gather.reshape(64, -1), scatter.reshape(64, -1)], axis=-1)


def forward_kernel(m, lens, x_in, taps, normed_out, slope_out, inv_out, act_out, *rest):
    x_ref, hid, mix, normed_ref, slope_ref, inv_ref, act, act_ref, sem, sems = rest
    length = lens[m]
    frames, feats = x_ref.shape
    cols = feats // LANES
    copy = pltpu.make_async_copy(x_in.at[m], x_ref, sem)
    copy.start()
    for c in range(cols):
        hid[c, 0:PAD, :] = jnp.zeros((PAD, LANES), F32)
        hid[c, PAD + frames : 2 * PAD + frames, :] = jnp.zeros((PAD, LANES), F32)
    copy.wait()

    def load(i, carry):
        r = pl.multiple_of(i * 16, 16)
        rows = r + lax.broadcasted_iota(jnp.int32, (16, LANES), 0)
        keep = rows < length
        for c in range(cols):
            v = x_ref[pl.ds(r, 16), c * LANES : (c + 1) * LANES].astype(F32)
            hid[c, pl.ds(r + PAD, 16), :] = jnp.where(keep, v, 0.0)
        return carry

    lax.fori_loop(0, frames // 16, load, 0, unroll=2)

    def conv(i, carry):
        r = pl.multiple_of(i * 64, 64)
        for c in range(cols):
            span = slice(c * LANES, (c + 1) * LANES)
            total = taps[0:1, span] * hid[c, pl.ds(r + PAD - 2, 64), :]
            for k in range(1, 5):
                total = total + taps[k : k + 1, span] * hid[c, pl.ds(r + PAD - 2 + k, 64), :]
            mix[pl.ds(r, 64), span] = total
        return carry

    lax.fori_loop(0, frames // 64, conv, 0)

    def norm(i, carry):
        r = pl.multiple_of(i * 16, 16)
        keep = r + lax.broadcasted_iota(jnp.int32, (16, 1), 0) < length
        mixed = mix[pl.ds(r, 16), :]
        centred = mixed - jnp.mean(mixed, axis=-1, keepdims=True)
        inverse = lax.rsqrt(jnp.mean(centred * centred, axis=-1, keepdims=True) + EPSILON)
        gain = taps[5:6, :]
        normed = centred * inverse
        gained = normed * gain
        logistic = jax.nn.sigmoid(gained)
        normed_ref[pl.ds(r, 16), :] = normed.astype(BF16)
        slope = (logistic + gained * logistic * (1.0 - logistic)) * gain
        slope_ref[pl.ds(r, 16), :] = jnp.where(keep, slope, 0.0).astype(BF16)
        act[pl.ds(r, 16), :] = jnp.where(keep, gained * logistic, 0.0).astype(BF16)
        inv_ref[pl.ds(r, 16), :] = jnp.broadcast_to(inverse, (16, LANES))
        return carry

    outs = ((normed_ref, normed_out), (slope_ref, slope_out), (inv_ref, inv_out))

    def quarter(q, carry):
        lax.fori_loop(0, frames // 64, lambda i, c: norm(q * (frames // 64) + i, c), 0, unroll=2)
        part = pl.ds(pl.multiple_of(q * (frames // 4), frames // 4), frames // 4)
        for n, (held, out) in enumerate(outs):
            pltpu.make_async_copy(held.at[part], out.at[part], sems.at[n]).start()
        return carry

    lax.fori_loop(0, 4, quarter, 0)
    for c in range(feats // 256):
        span = slice(c * 256, (c + 1) * 256)
        act_ref[span, :] = act[:, span].T
        pltpu.make_async_copy(act_ref.at[span], act_out.at[span], sems.at[3]).start()
    for n, (held, out) in enumerate(outs + ((act_ref, act_out),)):
        pltpu.make_async_copy(held, out, sems.at[n]).wait()


def forward(m, lens, x, taps):
    micro, frames, feats = x.shape
    return pl.pallas_call(
        functools.partial(forward_kernel, m),
        in_specs=[SMEM, HBM, VMEM],
        out_specs=[HBM] * 4,
        out_shape=[
            jax.ShapeDtypeStruct((frames, feats), BF16),
            jax.ShapeDtypeStruct((frames, feats), BF16),
            jax.ShapeDtypeStruct((frames, LANES), F32),
            jax.ShapeDtypeStruct((feats, frames), BF16),
        ],
        scratch_shapes=[
            pltpu.VMEM((frames, feats), BF16),
            pltpu.VMEM((feats // LANES, frames + 2 * PAD, LANES), F32),
            pltpu.VMEM((frames, feats), F32),
            pltpu.VMEM((frames, feats), BF16),
            pltpu.VMEM((frames, feats), BF16),
            pltpu.VMEM((frames, LANES), F32),
            pltpu.VMEM((frames, feats), BF16),
            pltpu.VMEM((feats, frames), BF16),
            pltpu.SemaphoreType.DMA,
            pltpu.SemaphoreType.DMA((4,)),
        ],
        compiler_params=params(60),
        cost_estimate=cost(8),
    )(lens, x, taps)


def relay_kernel(first, who, meta, grads, come, come_one, *rest):
    (wa, wb), rest = (rest[:4], rest[4:8]), rest[8:]
    (normed_in, slope_in, inv_in), taps, rest = (rest[0:2], rest[2:4], rest[4:6]), rest[6], rest[7:]
    if not first:
        rest = rest[2:]
    send, mixed_out, gain_out = rest[:3]
    w, up, normed, slope, inv, ga, gmix, narrow, out, gsum, low, high, sems = rest[3:]
    frames, feats = up.shape
    cols = feats // LANES
    half = feats // 2
    rows = 48
    section, place_x = meta[0], meta[3]
    turn = sum(jnp.where(section == i, m, 0) for i, m in enumerate(who))
    active, slot = turn >= 0, jnp.maximum(turn, 0)
    last, length = section == 3, meta[1 + slot]

    def pieces(group):
        made = []
        odd = (place_x + group) % 2
        for h, parts in enumerate((wa, wb)):
            for p in range(4):
                for j in range(4):
                    at = h * 32 + p * 8 + 2 * j + odd
                    place = pl.multiple_of(meta[8 + at] * rows, 16)
                    made.append(
                        pltpu.make_async_copy(
                            parts[p].at[2 * j + odd],
                            w.at[pl.ds(place, rows), pl.ds(h * half, half)],
                            sems.at[0 if group == 0 else 8],
                        )
                    )
        return made

    @pl.when(active)
    def _():
        @pl.when(last)
        def _():
            pltpu.make_async_copy(grads.at[slot], up, sems.at[1]).start()

        @pl.when(section == 1)
        def _():
            pltpu.make_async_copy(come_one, up, sems.at[1]).start()

        @pl.when(jnp.logical_and(section != 3, section != 1))
        def _():
            pltpu.make_async_copy(come, up, sems.at[1]).start()

        weights = [pieces(0), pieces(1)]
        for copy in weights[0]:
            copy.start()
        for m in range(2):

            @pl.when(slot == m)
            def _():
                pltpu.make_async_copy(slope_in[m], slope, sems.at[3]).start()
                pltpu.make_async_copy(normed_in[m], normed, sems.at[2]).start()
                pltpu.make_async_copy(inv_in[m], inv, sems.at[4]).start()

        for copy in weights[1]:
            copy.start()
        for c in range(cols):
            gmix[c, 0:PAD, :] = jnp.zeros((PAD, LANES), F32)
            gmix[c, PAD + frames : 2 * PAD + frames, :] = jnp.zeros((PAD, LANES), F32)
        low[...] = jnp.zeros_like(low)
        high[...] = jnp.zeros_like(high)

        def multiply(n):
            ga[:, n * 256 : (n + 1) * 256] = lax.dot_general(
                up[...],
                w[n * 256 : (n + 1) * 256, :],
                (((1,), (1,)), ((), ())),
                preferred_element_type=F32,
            )

        def weigh(n):
            span = slice(n * 256, (n + 1) * 256)
            total = jnp.zeros((8, 256), F32)
            for r in range(0, frames, 32):
                part = slice(r, r + 32)
                gn = ga[part, span] * slope[part, span].astype(F32)
                both = gn * normed[part, span].astype(F32)
                ga[part, span] = gn
                low[part, :] += gn[:, :LANES] + gn[:, LANES:]
                high[part, :] += both[:, :LANES] + both[:, LANES:]
                total = total + (both[:8] + both[8:16]) + (both[16:24] + both[24:])
            gsum[:, span] = total

        pltpu.make_async_copy(come, up, sems.at[1]).wait()
        for copy in weights[0]:
            copy.wait()
        multiply(0)
        pltpu.make_async_copy(slope_in[0], slope, sems.at[3]).wait()
        pltpu.make_async_copy(normed_in[0], normed, sems.at[2]).wait()
        pltpu.make_async_copy(inv_in[0], inv, sems.at[4]).wait()
        count = feats // 256
        for n in range(1, count):
            if n == count // 2:
                for copy in weights[1]:
                    copy.wait()
            multiply(n)
            weigh(n - 1)
        weigh(count - 1)
        gain_copy = pltpu.make_async_copy(gsum, gain_out.at[slot], sems.at[6])
        gain_copy.start()

        def means(i, carry):
            r = pl.multiple_of(i * 64, 64)
            for ref in (low, high):
                mean = jnp.sum(ref[pl.ds(r, 64), :], axis=-1, keepdims=True) * (1.0 / feats)
                ref[pl.ds(r, 64), :] = jnp.broadcast_to(mean, (64, LANES))
            return carry

        lax.fori_loop(0, frames // 64, means, 0, unroll=2)

        def finish(i, carry):
            r = pl.multiple_of(i * 16, 16)
            a, b, scale = low[pl.ds(r, 16), :], high[pl.ds(r, 16), :], inv[pl.ds(r, 16), :]
            for c in range(cols):
                span = slice(c * LANES, (c + 1) * LANES)
                nm = normed[pl.ds(r, 16), span].astype(F32)
                mixed = scale * (ga[pl.ds(r, 16), span] - a - nm * b)
                narrow[pl.ds(r, 16), span] = mixed.astype(BF16)
                gmix[c, pl.ds(r + PAD, 16), :] = mixed
            return carry

        lax.fori_loop(0, frames // 16, finish, 0, unroll=2)
        saved = pltpu.make_async_copy(narrow, mixed_out.at[slot], sems.at[5])
        saved.start()

        def conv(i, carry):
            r = pl.multiple_of(i * 64, 64)
            keep = r + lax.broadcasted_iota(jnp.int32, (64, LANES), 0) < length
            for c in range(cols):
                span = slice(c * LANES, (c + 1) * LANES)
                total = taps[4:5, span] * gmix[c, pl.ds(r + PAD - 2, 64), :]
                for k in range(1, 5):
                    total = total + taps[4 - k : 5 - k, span] * gmix[c, pl.ds(r + PAD - 2 + k, 64), :]
                result = up[pl.ds(r, 64), span].astype(F32) + jnp.where(keep, total, 0.0)
                out[pl.ds(r, 64), span] = result.astype(BF16)
            part = pl.ds(r, 64)
            pltpu.make_async_copy(out.at[part], send.at[part], sems.at[7]).start()
            return carry

        lax.fori_loop(0, frames // 64, conv, 0)
        pltpu.make_async_copy(out, send, sems.at[7]).wait()
        saved.wait()
        gain_copy.wait()


def relay(who, meta, grads, come, come_one, weights, saved, taps, state):
    micro, frames, feats = grads.shape
    cols = feats // LANES
    first = state is None
    shapes = [
        jax.ShapeDtypeStruct((frames, feats), BF16),
        jax.ShapeDtypeStruct((micro, frames, feats), BF16),
        jax.ShapeDtypeStruct((micro, 8, feats), F32),
    ]
    operands = [meta, grads, come, come_one, *weights, *saved, taps]
    specs = [SMEM, HBM, ANY, ANY] + [HBM] * (len(operands) - 5) + [VMEM]
    aliases = {}
    if not first:
        aliases = {len(operands) + i: 1 + i for i in range(2)}
        operands += list(state)
        specs += [HBM] * 2
    out = pl.pallas_call(
        functools.partial(relay_kernel, first, who),
        in_specs=specs,
        out_specs=[ANY] + [HBM] * 2,
        out_shape=shapes,
        input_output_aliases=aliases,
        scratch_shapes=[
            pltpu.VMEM((feats, feats), BF16),
            pltpu.VMEM((frames, feats), BF16),
            pltpu.VMEM((frames, feats), BF16),
            pltpu.VMEM((frames, feats), BF16),
            pltpu.VMEM((frames, LANES), F32),
            pltpu.VMEM((frames, feats), F32),
            pltpu.VMEM((cols, frames + 2 * PAD, LANES), F32),
            pltpu.VMEM((frames, feats), BF16),
            pltpu.VMEM((frames, feats), BF16),
            pltpu.VMEM((8, feats), F32),
            pltpu.VMEM((frames, LANES), F32),
            pltpu.VMEM((frames, LANES), F32),
            pltpu.SemaphoreType.DMA((10,)),
        ],
        compiler_params=params(60),
        cost_estimate=cost(1),
    )(*operands)
    return out[0], tuple(out[1:])


def weight_kernel(meta, act_a, act_b, *rest):
    sources, outs, (act, gm, acc, block, sems) = rest[:7], rest[7:15], rest[15:]
    feats, frames = act_a.shape
    half = feats // 2
    section = meta[0]
    copies = [
        pltpu.make_async_copy(act_a, act.at[:, pl.ds(0, frames)], sems.at[0]),
        pltpu.make_async_copy(act_b, act.at[:, pl.ds(frames, frames)], sems.at[1]),
    ]
    for copy in copies:
        copy.start()
    for m in range(2):
        for owner in range(4):

            @pl.when(section == owner)
            def _():
                source = sources[0].at[m] if owner == 3 else sources[1 + 2 * owner + m]
                place = gm.at[pl.ds(m * frames, frames)]
                pltpu.make_async_copy(source, place, sems.at[2 + m]).start()

    for m in range(2):
        copies[m].wait()
        pltpu.make_async_copy(sources[1], gm.at[pl.ds(m * frames, frames)], sems.at[2 + m]).wait()
    leaving = []
    rows = 48
    for h in range(2):

        def multiply(n, carry):
            r = pl.multiple_of(n * 384, 384)
            acc[...] = lax.dot_general(
                act[pl.ds(r, 384), :],
                gm[:, h * half : (h + 1) * half],
                (((1,), (0,)), ((), ())),
                preferred_element_type=F32,
            )
            for q in range(8):
                place = meta[72 + h * 32 + n * 8 + q]
                block[h, place] = acc[q * rows : (q + 1) * rows, :].astype(BF16)
            return carry

        lax.fori_loop(0, feats // 384, multiply, 0)
        for p in range(4):
            copy = pltpu.make_async_copy(
                block.at[h, pl.ds(p * 8, 8)], outs[h * 4 + p], sems.at[4 + h * 4 + p]
            )
            copy.start()
            leaving.append(copy)
    for copy in leaving:
        copy.wait()


def weight_terms(meta, acts, grads, comes):
    feats, frames = acts[0].shape
    half = feats // 2
    operands = [meta, *acts, grads, *comes]
    return pl.pallas_call(
        weight_kernel,
        in_specs=[SMEM, ANY, ANY, HBM] + [ANY] * len(comes),
        out_specs=[ANY] * 8,
        out_shape=[jax.ShapeDtypeStruct((8, 48, half), BF16)] * 8,
        scratch_shapes=[
            pltpu.VMEM((feats, 2 * frames), BF16),
            pltpu.VMEM((2 * frames, feats), BF16),
            pltpu.VMEM((384, half), F32),
            pltpu.VMEM((2, 32, 48, half), BF16),
            pltpu.SemaphoreType.DMA((12,)),
        ],
        compiler_params=params(60),
        cost_estimate=cost(8),
    )(*operands)


def tap_kernel(m, meta, x_in, mixed_in, gain_in, taps, *rest):
    count = 6 if m == 1 else 0
    sent, rest = rest[:count], rest[count:]
    if count:
        out, frame_out, x_ref, mixed_ref, gain_ref, hid, sems, held, more = rest
    else:
        out, x_ref, mixed_ref, gain_ref, hid, sems = rest
    section = meta[0]
    length = meta[1 + m]
    frames, feats = x_ref.shape
    cols = feats // LANES
    copies = [
        pltpu.make_async_copy(x_in.at[m], x_ref, sems.at[0]),
        pltpu.make_async_copy(mixed_in.at[m], mixed_ref, sems.at[1]),
        pltpu.make_async_copy(gain_in.at[m], gain_ref, sems.at[2]),
    ]
    for copy in copies:
        copy.start()
    if count:
        for owner, turns in enumerate(((4, 5), (3, 4), (1, 2), (0, 1))):

            @pl.when(section == owner)
            def _():
                for p in range(2):
                    pltpu.make_async_copy(sent[turns[p]], held.at[p], more.at[p]).start()

    for c in range(cols):
        hid[c, 0:PAD, :] = jnp.zeros((PAD, LANES), F32)
        hid[c, PAD + frames : 2 * PAD + frames, :] = jnp.zeros((PAD, LANES), F32)
    copies[0].wait()

    def load(i, carry):
        r = pl.multiple_of(i * 16, 16)
        keep = r + lax.broadcasted_iota(jnp.int32, (16, LANES), 0) < length
        for c in range(cols):
            v = x_ref[pl.ds(r, 16), c * LANES : (c + 1) * LANES].astype(F32)
            hid[c, pl.ds(r + PAD, 16), :] = jnp.where(keep, v, 0.0)
        return carry

    lax.fori_loop(0, frames // 16, load, 0, unroll=2)
    copies[1].wait()
    copies[2].wait()
    leave = None
    if count:
        for p in range(2):
            pltpu.make_async_copy(sent[0], held.at[p], more.at[p]).wait()
        leave = pltpu.make_async_copy(held, frame_out, more.at[2])
        leave.start()
    for c in range(cols):
        span = slice(c * LANES, (c + 1) * LANES)

        def add(i, sums):
            r = pl.multiple_of(i * 32, 32)
            grown = list(sums)
            wide = mixed_ref[pl.ds(r, 32), span].astype(F32)
            for q in range(4):
                g = wide[8 * q : 8 * q + 8]
                for k in range(5):
                    grown[k] = grown[k] + g * hid[c, pl.ds(r + PAD - 2 + k + 8 * q, 8), :]
            return tuple(grown)

        sums = lax.fori_loop(0, frames // 32, add, (jnp.zeros((8, LANES), F32),) * 5, unroll=2)
        for k in range(5):
            out[k : k + 1, span] = jnp.sum(sums[k], axis=0, keepdims=True)
    out[5:6, :] = jnp.sum(gain_ref[...], axis=0, keepdims=True) / taps[5:6, :]
    out[6:8, :] = jnp.zeros((2, feats), F32)
    if count:
        leave.wait()


def tap_terms(m, meta, x, mixed, gain, taps, sent):
    micro, frames, feats = x.shape
    more = len(sent) > 0
    made = pl.pallas_call(
        functools.partial(tap_kernel, m),
        in_specs=[SMEM, HBM, HBM, HBM, VMEM] + [HBM] * len(sent),
        out_specs=[VMEM] + [HBM] * more,
        out_shape=[jax.ShapeDtypeStruct((8, feats), F32)]
        + [jax.ShapeDtypeStruct(x.shape, BF16)] * more,
        scratch_shapes=[
            pltpu.VMEM((frames, feats), BF16),
            pltpu.VMEM((frames, feats), BF16),
            pltpu.VMEM((8, feats), F32),
            pltpu.VMEM((feats // LANES, frames + 2 * PAD, LANES), F32),
            pltpu.SemaphoreType.DMA((3,)),
        ]
        + [pltpu.VMEM(x.shape, BF16), pltpu.SemaphoreType.DMA((3,))] * more,
        compiler_params=params(60),
        cost_estimate=cost(5),
    )(meta, x, mixed, gain, taps, *sent)
    return made[0], (made[1] if more else None)


def shift(x, axis, d):
    n = lax.axis_size(axis)
    return lax.ppermute(x, axis, [(i, (i + d) % n) for i in range(n)])


def by_core(first, second):
    return jnp.where(lax.axis_index("section") % 2 == 0, first, second)


def shift_on(first, second, axis):
    n = lax.axis_size(axis)
    route = [
        (s * n + i, s * n + (i + (1 if s % 2 == 0 else -1)) % n)
        for s in range(lax.axis_size("section"))
        for i in range(n)
    ]
    return lax.ppermute(by_core(first, second), ("section", axis), route)


def swap(x, axis, d):
    n = lax.axis_size(axis)
    return lax.ppermute(x, axis, [(i, i ^ d) for i in range(n)])


def gather_weights(shard, small):
    rows, width = shard.shape
    half = width // 2
    extra = jnp.zeros((16, half), BF16).at[0, : small.size].set(small.reshape(-1))
    own = [jnp.concatenate([shard[:, :half], extra]), shard[:, half:]]
    pairs = [jnp.stack([p, swap(p, "xh", 1)]) for p in own]

    def near(p, axis):
        return [p] + [shift(p, axis, d) for d in (1, -1, 2)]

    first = [jnp.concatenate(near(p, a)) for p, a in zip(pairs, ("y", "z"))]
    packed = first[0][:, rows, : small.size]
    packed = jnp.stack(near(packed, "z"))
    packed = packed.reshape(4, 4, 2, *small.shape)
    packed = jnp.stack([packed[i] for i in (0, 2, 3, 1)])
    packed = jnp.stack([packed[:, i] for i in (0, 2, 3, 1)], axis=1)
    x, z, y = (lax.axis_index(a) for a in ("xh", "z", "y"))
    packed = jnp.tile(packed, (2, 2, 2, 1, 1))
    zero = jnp.zeros((), jnp.int32)
    packed = lax.dynamic_slice(
        packed, ((4 - z) % 4, (4 - y) % 4, (2 - x) % 2, zero, zero), (4, 4, 2, *small.shape)
    )
    whole = packed.transpose(3, 2, 0, 1, 4).reshape(small.shape[0], width)

    def ring(own, axis):
        left, right = shift(own, axis, 1), shift(own, axis, -1)
        return own, left, right, shift_on(left, right, axis)

    pieces = [ring(p[:, :rows], a) for p, a in zip(first, ("z", "y"))]
    return [*pieces[0], *pieces[1]], whole


def scatter_near(pieces, axis):
    total = pieces[0]
    for d in (1, 2, 3):
        total = total + shift(pieces[d].astype(BF16), axis, d).astype(F32)
    return total


def scatter_weights(parts, terms):
    rings = (parts[:4], "z"), (parts[4:], "y")
    moved = [(shift(p[0], a, 1), shift(p[1], a, -1)) for p, a in rings]
    moved, terms = lax.optimization_barrier((moved, terms))
    halves = []
    for (group, axis), (p, q) in zip(rings, moved):
        far, near = by_core(p, q), by_core(q, p)
        onward = (group[2].astype(F32) + far.astype(F32)).astype(BF16)
        come = shift_on(onward, onward, axis)
        halves.append(group[3].astype(F32) + near.astype(F32) + come.astype(F32))
    a, b = halves
    packed = scatter_near(terms, "z")
    extra = jnp.zeros((8, 16, a.shape[2]), F32).at[:, 0, : packed.shape[1]].set(packed)
    a = jnp.concatenate([a, extra], axis=1)
    own = []
    for blocks, axis in ((a, "y"), (b, "z")):
        pieces = [blocks[2 * i : 2 * i + 2] for i in range(4)]
        summed = scatter_near(pieces, axis)
        own.append(summed[0] + swap(summed[1].astype(BF16), "xh", 1).astype(F32))
    rows = own[1].shape[0]
    return jnp.concatenate([own[0][:rows], own[1]], axis=1), own[0][rows, : packed.shape[1]]


def body(saved_inputs, grad_outputs, lengths, pointwise, depth_kernel, norm_gain):
    section = lax.axis_index("section")
    x, z, y = (lax.axis_index(a) for a in ("xh", "z", "y"))
    inputs = saved_inputs[0, :, 0]
    grads = grad_outputs[:, 0]
    lens = lengths[:, 0]
    micro, frames, features = inputs.shape
    factor = float(32 * micro * frames) ** (-0.5)

    at = section % 2 * 32 + x * 16 + z * 4 + y
    table = lax.dynamic_index_in_dim(jnp.asarray(tables()), at, 0, keepdims=False)
    meta = jnp.concatenate([section[None], lens, x[None], jnp.zeros((4,), jnp.int32), table])

    small = jnp.concatenate([depth_kernel[0], norm_gain[0:1]], axis=0)
    weights, small = gather_weights(pointwise[0], small)
    taps = jnp.pad(small.astype(F32), ((0, 2), (0, 0)))
    made = [forward(0, lens, inputs, taps)] * 2

    def turn(state, come, come_one, who):
        saved = [made[m][i] for i in range(3) for m in range(2)]
        return relay(who, meta, grads, come, come_one, weights, saved, taps, state)

    def hop(block, source):
        return lax.ppermute(block, "section", [(source, source - 1)])

    outs = [None] * 6
    outs[0], state = turn(None, made[0][0], made[0][0], (-1, -1, -1, 0))
    two_0 = hop(outs[0], 3)
    later, _ = lax.optimization_barrier((taps, outs[0]))
    made[1] = forward(1, lens, inputs, later)
    acts = [made[0][3], made[1][3]]
    outs[1], state = turn(state, two_0, two_0, (-1, -1, 0, 1))
    two_1, one_0 = hop(outs[1], 3), hop(outs[1], 2)
    outs[2], state = turn(state, two_1, two_1, (-1, -1, 1, -1))
    one_1 = hop(outs[2], 2)
    outs[3], state = turn(state, one_0, one_0, (-1, 0, -1, -1))
    outs[3], one_1 = lax.optimization_barrier((outs[3], one_1))
    zero_0 = hop(outs[3], 1)
    outs[4], state = turn(state, zero_0, one_1, (0, 1, -1, -1))
    zero_1 = hop(outs[4], 1)
    sums_0, _ = tap_terms(0, meta, inputs, *state, taps, outs[:0])
    zero_1, sums_0 = lax.optimization_barrier((zero_1, sums_0))
    parts = weight_terms(meta, acts, grads, [zero_0, zero_1, one_0, one_1, two_0, two_1])
    outs[5], state = turn(state, zero_1, zero_1, (1, -1, -1, -1))
    sums_1, frame_out = tap_terms(1, meta, inputs, *state, taps, outs)
    sums = sums_0 + sums_1

    def terms():
        blocks = (sums[:6] * factor).reshape(6, 2, 4, 4, 48)
        blocks = blocks.transpose(2, 3, 1, 0, 4).reshape(4, 4, 2, 288)
        blocks = lax.dynamic_slice(
            jnp.tile(blocks, (2, 2, 2, 1)), (z, y, x, jnp.zeros((), jnp.int32)), (4, 4, 2, 288)
        )
        return jnp.stack([blocks[:, i, r] for i, r in SCATTERED], axis=1)

    point_share, share = scatter_weights(parts, terms())
    share = share.reshape(6, 48)
    return (
        frame_out[None, :, None],
        (point_share * factor)[None],
        share[None, :5],
        share[5:6],
    )


def solution(mesh):
    fine = Mesh(mesh.devices.reshape(4, 2, 4, 4), ("section", "xh", "z", "y"))
    fsdp = ("xh", "z", "y")
    return jax.shard_map(
        body,
        mesh=fine,
        in_specs=(
            P("section", None, fsdp, None, None),
            P(None, fsdp, None, None),
            P(None, fsdp),
            P("section", fsdp, None),
            P("section", None, fsdp),
            P("section", fsdp),
        ),
        out_specs=(
            P("section", None, fsdp, None, None),
            P("section", fsdp, None),
            P("section", None, fsdp),
            P("section", fsdp),
        ),
        check_vma=False,
    )
```

```python
import functools

import jax
import jax.numpy as jnp
import numpy as np
from jax import lax
from jax.experimental import pallas as pl
from jax.experimental.pallas import tpu as pltpu
from jax.sharding import Mesh
from jax.sharding import PartitionSpec as P

EPSILON = 1e-05
F32 = jnp.float32
BF16 = jnp.bfloat16
LANES = 128
PAD = 8
ANY = pl.BlockSpec(memory_space=pl.ANY)
HBM = pl.BlockSpec(memory_space=pltpu.HBM)
SMEM = pl.BlockSpec(memory_space=pltpu.SMEM)
VMEM = pl.BlockSpec(memory_space=pltpu.VMEM)

def params(limit, **kw):
    return pltpu.CompilerParams(vmem_limit_bytes=limit << 20, **kw)


def cost(us):
    return pl.CostEstimate(flops=int(us * 1.0e9), bytes_accessed=1 << 20, transcendentals=0)


def partners(core):
    near, mirrored = [i ^ 1 for i in range(4)], [3 - i for i in range(4)]
    return (near, mirrored) if core == 0 else (mirrored, near)


def tables():
    gather = np.zeros((2, 2, 4, 4, 2, 4, 4, 2), np.int32)
    scatter = np.zeros((2, 2, 4, 4, 2, 32), np.int32)
    for core, x, z, y, half in np.ndindex(2, 2, 4, 4, 2):
        inner, outer = (y, z) if half == 0 else (z, y)
        one, two = partners(core)

        def block(a, b, r):
            zz, yy = (a, b) if half == 0 else (b, a)
            return (x + r) % 2 * 16 + zz * 4 + yy

        def order(me):
            return me, one[me], two[me], one[two[me]]

        for o, a in enumerate(order(outer)):
            for i, b in enumerate(order(inner)):
                for r in range(2):
                    gather[core, x, z, y, half, o, i, r] = block(a, b, r)
                    at = (3, 1, 2, 0)
                    place = at.index(o) * 8 + at.index(i) * 2 + r
                    scatter[core, x, z, y, half, block(a, b, r)] = place
    return np.concatenate([gather.reshape(64, -1), scatter.reshape(64, -1)], axis=-1)


def forward_kernel(m, lens, x_in, taps, normed_out, slope_out, inv_out, act_out, *rest):
    x_ref, hid, mix, normed_ref, slope_ref, inv_ref, act, act_ref, sem, sems = rest
    length = lens[m]
    frames, feats = x_ref.shape
    cols = feats // LANES
    copy = pltpu.make_async_copy(x_in.at[m], x_ref, sem)
    copy.start()
    for c in range(cols):
        hid[c, 0:PAD, :] = jnp.zeros((PAD, LANES), F32)
        hid[c, PAD + frames : 2 * PAD + frames, :] = jnp.zeros((PAD, LANES), F32)
    copy.wait()

    def load(i, carry):
        r = pl.multiple_of(i * 16, 16)
        rows = r + lax.broadcasted_iota(jnp.int32, (16, LANES), 0)
        keep = rows < length
        for c in range(cols):
            v = x_ref[pl.ds(r, 16), c * LANES : (c + 1) * LANES].astype(F32)
            hid[c, pl.ds(r + PAD, 16), :] = jnp.where(keep, v, 0.0)
        return carry

    lax.fori_loop(0, frames // 16, load, 0, unroll=2)

    def conv(i, carry):
        r = pl.multiple_of(i * 64, 64)
        for c in range(cols):
            span = slice(c * LANES, (c + 1) * LANES)
            total = taps[0:1, span] * hid[c, pl.ds(r + PAD - 2, 64), :]
            for k in range(1, 5):
                total = total + taps[k : k + 1, span] * hid[c, pl.ds(r + PAD - 2 + k, 64), :]
            mix[pl.ds(r, 64), span] = total
        return carry

    lax.fori_loop(0, frames // 64, conv, 0)

    def norm(i, carry):
        r = pl.multiple_of(i * 16, 16)
        keep = r + lax.broadcasted_iota(jnp.int32, (16, 1), 0) < length
        mixed = mix[pl.ds(r, 16), :]
        centred = mixed - jnp.mean(mixed, axis=-1, keepdims=True)
        inverse = lax.rsqrt(jnp.mean(centred * centred, axis=-1, keepdims=True) + EPSILON)
        gain = taps[5:6, :]
        normed = centred * inverse
        gained = normed * gain
        logistic = jax.nn.sigmoid(gained)
        normed_ref[pl.ds(r, 16), :] = normed.astype(BF16)
        slope = (logistic + gained * logistic * (1.0 - logistic)) * gain
        slope_ref[pl.ds(r, 16), :] = jnp.where(keep, slope, 0.0).astype(BF16)
        act[pl.ds(r, 16), :] = jnp.where(keep, gained * logistic, 0.0).astype(BF16)
        inv_ref[pl.ds(r, 16), :] = jnp.broadcast_to(inverse, (16, LANES))
        return carry

    outs = ((normed_ref, normed_out), (slope_ref, slope_out), (inv_ref, inv_out))

    def quarter(q, carry):
        lax.fori_loop(0, frames // 64, lambda i, c: norm(q * (frames // 64) + i, c), 0, unroll=2)
        part = pl.ds(pl.multiple_of(q * (frames // 4), frames // 4), frames // 4)
        for n, (held, out) in enumerate(outs):
            pltpu.make_async_copy(held.at[part], out.at[part], sems.at[n]).start()
        return carry

    lax.fori_loop(0, 4, quarter, 0)
    for c in range(feats // 256):
        span = slice(c * 256, (c + 1) * 256)
        act_ref[span, :] = act[:, span].T
        pltpu.make_async_copy(act_ref.at[span], act_out.at[span], sems.at[3]).start()
    for n, (held, out) in enumerate(outs + ((act_ref, act_out),)):
        pltpu.make_async_copy(held, out, sems.at[n]).wait()


def forward(m, lens, x, taps):
    micro, frames, feats = x.shape
    return pl.pallas_call(
        functools.partial(forward_kernel, m),
        in_specs=[SMEM, HBM, VMEM],
        out_specs=[HBM] * 4,
        out_shape=[
            jax.ShapeDtypeStruct((frames, feats), BF16),
            jax.ShapeDtypeStruct((frames, feats), BF16),
            jax.ShapeDtypeStruct((frames, LANES), F32),
            jax.ShapeDtypeStruct((feats, frames), BF16),
        ],
        scratch_shapes=[
            pltpu.VMEM((frames, feats), BF16),
            pltpu.VMEM((feats // LANES, frames + 2 * PAD, LANES), F32),
            pltpu.VMEM((frames, feats), F32),
            pltpu.VMEM((frames, feats), BF16),
            pltpu.VMEM((frames, feats), BF16),
            pltpu.VMEM((frames, LANES), F32),
            pltpu.VMEM((frames, feats), BF16),
            pltpu.VMEM((feats, frames), BF16),
            pltpu.SemaphoreType.DMA,
            pltpu.SemaphoreType.DMA((4,)),
        ],
        compiler_params=params(60),
        cost_estimate=cost(8),
    )(lens, x, taps)


def relay_kernel(first, who, meta, grads, come, come_one, *rest):
    (wa, wb), rest = (rest[:2], rest[2:4]), rest[4:]
    (normed_in, slope_in, inv_in), taps, rest = (rest[0:2], rest[2:4], rest[4:6]), rest[6], rest[7:]
    if not first:
        rest = rest[2:]
    send, mixed_out, gain_out = rest[:3]
    w, up, normed, slope, inv, ga, gmix, narrow, out, gsum, low, high, sems = rest[3:]
    frames, feats = up.shape
    cols = feats // LANES
    half = feats // 2
    rows = 48
    section, place_x = meta[0], meta[3]
    turn = sum(jnp.where(section == i, m, 0) for i, m in enumerate(who))
    active, slot = turn >= 0, jnp.maximum(turn, 0)
    last, length = section == 3, meta[1 + slot]

    def pieces(group):
        made = []
        odd = (place_x + group) % 2
        for h, parts in enumerate((wa, wb)):
            for p in range(2):
                for j in range(8):
                    at = h * 32 + p * 16 + 2 * j + odd
                    place = pl.multiple_of(meta[8 + at] * rows, 16)
                    made.append(
                        pltpu.make_async_copy(
                            parts[p].at[2 * j + odd],
                            w.at[pl.ds(place, rows), pl.ds(h * half, half)],
                            sems.at[0 if group == 0 else 8],
                        )
                    )
        return made

    @pl.when(active)
    def _():
        @pl.when(last)
        def _():
            pltpu.make_async_copy(grads.at[slot], up, sems.at[1]).start()

        @pl.when(section == 1)
        def _():
            pltpu.make_async_copy(come_one, up, sems.at[1]).start()

        @pl.when(jnp.logical_and(section != 3, section != 1))
        def _():
            pltpu.make_async_copy(come, up, sems.at[1]).start()

        weights = [pieces(0), pieces(1)]
        for copy in weights[0]:
            copy.start()
        for m in range(2):

            @pl.when(slot == m)
            def _():
                pltpu.make_async_copy(slope_in[m], slope, sems.at[3]).start()
                pltpu.make_async_copy(normed_in[m], normed, sems.at[2]).start()
                pltpu.make_async_copy(inv_in[m], inv, sems.at[4]).start()

        for copy in weights[1]:
            copy.start()
        for c in range(cols):
            gmix[c, 0:PAD, :] = jnp.zeros((PAD, LANES), F32)
            gmix[c, PAD + frames : 2 * PAD + frames, :] = jnp.zeros((PAD, LANES), F32)
        low[...] = jnp.zeros_like(low)
        high[...] = jnp.zeros_like(high)

        def multiply(n):
            ga[:, n * 256 : (n + 1) * 256] = lax.dot_general(
                up[...],
                w[n * 256 : (n + 1) * 256, :],
                (((1,), (1,)), ((), ())),
                preferred_element_type=F32,
            )

        def weigh(n):
            span = slice(n * 256, (n + 1) * 256)
            total = jnp.zeros((8, 256), F32)
            for r in range(0, frames, 32):
                part = slice(r, r + 32)
                gn = ga[part, span] * slope[part, span].astype(F32)
                both = gn * normed[part, span].astype(F32)
                ga[part, span] = gn
                low[part, :] += gn[:, :LANES] + gn[:, LANES:]
                high[part, :] += both[:, :LANES] + both[:, LANES:]
                total = total + (both[:8] + both[8:16]) + (both[16:24] + both[24:])
            gsum[:, span] = total

        pltpu.make_async_copy(come, up, sems.at[1]).wait()
        for copy in weights[0]:
            copy.wait()
        multiply(0)
        pltpu.make_async_copy(slope_in[0], slope, sems.at[3]).wait()
        pltpu.make_async_copy(normed_in[0], normed, sems.at[2]).wait()
        pltpu.make_async_copy(inv_in[0], inv, sems.at[4]).wait()
        count = feats // 256
        for n in range(1, count):
            if n == count // 2:
                for copy in weights[1]:
                    copy.wait()
            multiply(n)
            weigh(n - 1)
        weigh(count - 1)
        gain_copy = pltpu.make_async_copy(gsum, gain_out.at[slot], sems.at[6])
        gain_copy.start()

        def means(i, carry):
            r = pl.multiple_of(i * 64, 64)
            for ref in (low, high):
                mean = jnp.sum(ref[pl.ds(r, 64), :], axis=-1, keepdims=True) * (1.0 / feats)
                ref[pl.ds(r, 64), :] = jnp.broadcast_to(mean, (64, LANES))
            return carry

        lax.fori_loop(0, frames // 64, means, 0, unroll=2)

        def finish(i, carry):
            r = pl.multiple_of(i * 16, 16)
            a, b, scale = low[pl.ds(r, 16), :], high[pl.ds(r, 16), :], inv[pl.ds(r, 16), :]
            for c in range(cols):
                span = slice(c * LANES, (c + 1) * LANES)
                nm = normed[pl.ds(r, 16), span].astype(F32)
                mixed = scale * (ga[pl.ds(r, 16), span] - a - nm * b)
                narrow[pl.ds(r, 16), span] = mixed.astype(BF16)
                gmix[c, pl.ds(r + PAD, 16), :] = mixed
            return carry

        lax.fori_loop(0, frames // 16, finish, 0, unroll=2)
        saved = pltpu.make_async_copy(narrow, mixed_out.at[slot], sems.at[5])
        saved.start()

        def conv(i, carry):
            r = pl.multiple_of(i * 64, 64)
            keep = r + lax.broadcasted_iota(jnp.int32, (64, LANES), 0) < length
            for c in range(cols):
                span = slice(c * LANES, (c + 1) * LANES)
                total = taps[4:5, span] * gmix[c, pl.ds(r + PAD - 2, 64), :]
                for k in range(1, 5):
                    total = total + taps[4 - k : 5 - k, span] * gmix[c, pl.ds(r + PAD - 2 + k, 64), :]
                result = up[pl.ds(r, 64), span].astype(F32) + jnp.where(keep, total, 0.0)
                out[pl.ds(r, 64), span] = result.astype(BF16)
            part = pl.ds(r, 64)
            pltpu.make_async_copy(out.at[part], send.at[part], sems.at[7]).start()
            return carry

        lax.fori_loop(0, frames // 64, conv, 0)
        pltpu.make_async_copy(out, send, sems.at[7]).wait()
        saved.wait()
        gain_copy.wait()


def relay(who, meta, grads, come, come_one, weights, saved, taps, state):
    micro, frames, feats = grads.shape
    cols = feats // LANES
    first = state is None
    shapes = [
        jax.ShapeDtypeStruct((frames, feats), BF16),
        jax.ShapeDtypeStruct((micro, frames, feats), BF16),
        jax.ShapeDtypeStruct((micro, 8, feats), F32),
    ]
    operands = [meta, grads, come, come_one, *weights, *saved, taps]
    specs = [SMEM, HBM, ANY, ANY] + [HBM] * (len(operands) - 5) + [VMEM]
    aliases = {}
    if not first:
        aliases = {len(operands) + i: 1 + i for i in range(2)}
        operands += list(state)
        specs += [HBM] * 2
    out = pl.pallas_call(
        functools.partial(relay_kernel, first, who),
        in_specs=specs,
        out_specs=[ANY] + [HBM] * 2,
        out_shape=shapes,
        input_output_aliases=aliases,
        scratch_shapes=[
            pltpu.VMEM((feats, feats), BF16),
            pltpu.VMEM((frames, feats), BF16),
            pltpu.VMEM((frames, feats), BF16),
            pltpu.VMEM((frames, feats), BF16),
            pltpu.VMEM((frames, LANES), F32),
            pltpu.VMEM((frames, feats), F32),
            pltpu.VMEM((cols, frames + 2 * PAD, LANES), F32),
            pltpu.VMEM((frames, feats), BF16),
            pltpu.VMEM((frames, feats), BF16),
            pltpu.VMEM((8, feats), F32),
            pltpu.VMEM((frames, LANES), F32),
            pltpu.VMEM((frames, LANES), F32),
            pltpu.SemaphoreType.DMA((10,)),
        ],
        compiler_params=params(60),
        cost_estimate=cost(1),
    )(*operands)
    return out[0], tuple(out[1:])


def weight_kernel(meta, act_a, act_b, *rest):
    sources, outs, (act, gm, acc, block, sems) = rest[:7], rest[7:11], rest[11:]
    feats, frames = act_a.shape
    half = feats // 2
    section = meta[0]
    copies = [
        pltpu.make_async_copy(act_a, act.at[:, pl.ds(0, frames)], sems.at[0]),
        pltpu.make_async_copy(act_b, act.at[:, pl.ds(frames, frames)], sems.at[1]),
    ]
    for copy in copies:
        copy.start()
    for m in range(2):
        for owner in range(4):

            @pl.when(section == owner)
            def _():
                source = sources[0].at[m] if owner == 3 else sources[1 + 2 * owner + m]
                place = gm.at[pl.ds(m * frames, frames)]
                pltpu.make_async_copy(source, place, sems.at[2 + m]).start()

    for m in range(2):
        copies[m].wait()
        pltpu.make_async_copy(sources[1], gm.at[pl.ds(m * frames, frames)], sems.at[2 + m]).wait()
    leaving = []
    rows = 48
    for h in range(2):

        def multiply(n, carry):
            r = pl.multiple_of(n * 384, 384)
            acc[...] = lax.dot_general(
                act[pl.ds(r, 384), :],
                gm[:, h * half : (h + 1) * half],
                (((1,), (0,)), ((), ())),
                preferred_element_type=F32,
            )
            for q in range(8):
                place = meta[72 + h * 32 + n * 8 + q]
                block[h, place] = acc[q * rows : (q + 1) * rows, :].astype(BF16)
            return carry

        lax.fori_loop(0, feats // 384, multiply, 0)
        for p in range(2):
            copy = pltpu.make_async_copy(
                block.at[h, pl.ds(p * 16, 16)], outs[h * 2 + p], sems.at[4 + h * 2 + p]
            )
            copy.start()
            leaving.append(copy)
    for copy in leaving:
        copy.wait()


def weight_terms(meta, acts, grads, comes):
    feats, frames = acts[0].shape
    half = feats // 2
    operands = [meta, *acts, grads, *comes]
    return pl.pallas_call(
        weight_kernel,
        in_specs=[SMEM, ANY, ANY, HBM] + [ANY] * len(comes),
        out_specs=[ANY] * 4,
        out_shape=[jax.ShapeDtypeStruct((16, 48, half), BF16)] * 4,
        scratch_shapes=[
            pltpu.VMEM((feats, 2 * frames), BF16),
            pltpu.VMEM((2 * frames, feats), BF16),
            pltpu.VMEM((384, half), F32),
            pltpu.VMEM((2, 32, 48, half), BF16),
            pltpu.SemaphoreType.DMA((12,)),
        ],
        compiler_params=params(60),
        cost_estimate=cost(8),
    )(*operands)


def tap_kernel(m, meta, x_in, mixed_in, gain_in, taps, *rest):
    count = 6 if m == 1 else 0
    sent, rest = rest[:count], rest[count:]
    if count:
        out, frame_out, x_ref, mixed_ref, gain_ref, hid, sems, held, more = rest
    else:
        out, x_ref, mixed_ref, gain_ref, hid, sems = rest
    section = meta[0]
    length = meta[1 + m]
    frames, feats = x_ref.shape
    cols = feats // LANES
    copies = [
        pltpu.make_async_copy(x_in.at[m], x_ref, sems.at[0]),
        pltpu.make_async_copy(mixed_in.at[m], mixed_ref, sems.at[1]),
        pltpu.make_async_copy(gain_in.at[m], gain_ref, sems.at[2]),
    ]
    for copy in copies:
        copy.start()
    if count:
        for owner, turns in enumerate(((4, 5), (3, 4), (1, 2), (0, 1))):

            @pl.when(section == owner)
            def _():
                for p in range(2):
                    pltpu.make_async_copy(sent[turns[p]], held.at[p], more.at[p]).start()

    for c in range(cols):
        hid[c, 0:PAD, :] = jnp.zeros((PAD, LANES), F32)
        hid[c, PAD + frames : 2 * PAD + frames, :] = jnp.zeros((PAD, LANES), F32)
    copies[0].wait()

    def load(i, carry):
        r = pl.multiple_of(i * 16, 16)
        keep = r + lax.broadcasted_iota(jnp.int32, (16, LANES), 0) < length
        for c in range(cols):
            v = x_ref[pl.ds(r, 16), c * LANES : (c + 1) * LANES].astype(F32)
            hid[c, pl.ds(r + PAD, 16), :] = jnp.where(keep, v, 0.0)
        return carry

    lax.fori_loop(0, frames // 16, load, 0, unroll=2)
    copies[1].wait()
    copies[2].wait()
    leave = None
    if count:
        for p in range(2):
            pltpu.make_async_copy(sent[0], held.at[p], more.at[p]).wait()
        leave = pltpu.make_async_copy(held, frame_out, more.at[2])
        leave.start()
    for c in range(cols):
        span = slice(c * LANES, (c + 1) * LANES)

        def add(i, sums):
            r = pl.multiple_of(i * 32, 32)
            grown = list(sums)
            wide = mixed_ref[pl.ds(r, 32), span].astype(F32)
            for q in range(4):
                g = wide[8 * q : 8 * q + 8]
                for k in range(5):
                    grown[k] = grown[k] + g * hid[c, pl.ds(r + PAD - 2 + k + 8 * q, 8), :]
            return tuple(grown)

        sums = lax.fori_loop(0, frames // 32, add, (jnp.zeros((8, LANES), F32),) * 5, unroll=2)
        for k in range(5):
            out[k : k + 1, span] = jnp.sum(sums[k], axis=0, keepdims=True)
    out[5:6, :] = jnp.sum(gain_ref[...], axis=0, keepdims=True) / taps[5:6, :]
    out[6:8, :] = jnp.zeros((2, feats), F32)
    if count:
        leave.wait()


def tap_terms(m, meta, x, mixed, gain, taps, sent):
    micro, frames, feats = x.shape
    more = len(sent) > 0
    made = pl.pallas_call(
        functools.partial(tap_kernel, m),
        in_specs=[SMEM, HBM, HBM, HBM, VMEM] + [HBM] * len(sent),
        out_specs=[VMEM] + [HBM] * more,
        out_shape=[jax.ShapeDtypeStruct((8, feats), F32)]
        + [jax.ShapeDtypeStruct(x.shape, BF16)] * more,
        scratch_shapes=[
            pltpu.VMEM((frames, feats), BF16),
            pltpu.VMEM((frames, feats), BF16),
            pltpu.VMEM((8, feats), F32),
            pltpu.VMEM((feats // LANES, frames + 2 * PAD, LANES), F32),
            pltpu.SemaphoreType.DMA((3,)),
        ]
        + [pltpu.VMEM(x.shape, BF16), pltpu.SemaphoreType.DMA((3,))] * more,
        compiler_params=params(60),
        cost_estimate=cost(5),
    )(meta, x, mixed, gain, taps, *sent)
    return made[0], (made[1] if more else None)


def swap(x, axis, d):
    n = lax.axis_size(axis)
    return lax.ppermute(x, axis, [(i, i ^ d) for i in range(n)])


def meet(x, axis, step):
    n = lax.axis_size(axis)
    route = [
        (s * n + i, s * n + partners(s % 2)[step][i])
        for s in range(lax.axis_size("section"))
        for i in range(n)
    ]
    return lax.ppermute(x, ("section", axis), route)


def gather_weights(shard, small):
    rows, width = shard.shape
    half = width // 2
    extra = jnp.concatenate([small[:, :half], small[:, half:]])
    own = [jnp.concatenate([shard[:, :half], extra]), shard[:, half:]]
    axes = ("y", "z")
    pieces = [jnp.stack([p, swap(p, "xh", 1)]) for p in own]
    for step in range(2):
        pieces = [jnp.concatenate([p, meet(p, a, step)]) for p, a in zip(pieces, axes)]
    small = jnp.sum(pieces[0][:, rows:].astype(F32), axis=0).astype(BF16)
    pieces = [p[:, :rows] for p in pieces]
    small, pieces = lax.optimization_barrier((small, pieces))
    come = [meet(p, a, 0) for p, a in zip(pieces, axes[::-1])]
    for step in range(2):
        small = small + meet(small, "z", step)
    small, come = lax.optimization_barrier((small, come))
    pieces = [jnp.concatenate([p, c]) for p, c in zip(pieces, come)]
    pieces = [(p, meet(p, a, 1)) for p, a in zip(pieces, axes[::-1])]
    whole = jnp.concatenate([small[:8], small[8:]], axis=1)
    return [*pieces[0], *pieces[1]], whole


def scatter_weights(parts, sums):
    axes = ("z", "y")
    sent, kept = parts[0::2], parts[1::2]
    moved = [meet(p, a, 0) for p, a in zip(sent, axes)]
    moved, sums = lax.optimization_barrier((moved, sums))
    half = sums.shape[1] // 2
    sums = jnp.concatenate([sums[:, :half], sums[:, half:]])
    grown = [k.astype(F32) + m.astype(F32) for k, m in zip(kept, moved)]
    onward = [g[:8].astype(BF16) for g in grown]
    onward, sums = lax.optimization_barrier((onward, sums))
    come = [meet(o, a, 1) for o, a in zip(onward, axes)]
    for step in range(2):
        sums = sums + meet(sums, "z", step)
    sums, come = lax.optimization_barrier((sums, come))
    blocks = [g[8:] + c.astype(F32) for g, c in zip(grown, come)]
    blocks[0] = jnp.concatenate([blocks[0], jnp.broadcast_to(sums, (8,) + sums.shape)], axis=1)
    own = []
    for b, axis in zip(blocks, axes[::-1]):
        b = b[4:] + meet(b[:4].astype(BF16), axis, 0).astype(F32)
        b = b[2:] + meet(b[:2].astype(BF16), axis, 1).astype(F32)
        own.append(b[0] + swap(b[1].astype(BF16), "xh", 1).astype(F32))
    rows = own[1].shape[0]
    sums = own[0][rows:]
    sums = jnp.concatenate([sums[:8], sums[8:]], axis=1)
    return jnp.concatenate([own[0][:rows], own[1]], axis=1), sums


def body(saved_inputs, grad_outputs, lengths, pointwise, depth_kernel, norm_gain):
    section = lax.axis_index("section")
    x, z, y = (lax.axis_index(a) for a in ("xh", "z", "y"))
    inputs = saved_inputs[0, :, 0]
    grads = grad_outputs[:, 0]
    lens = lengths[:, 0]
    micro, frames, features = inputs.shape
    factor = float(32 * micro * frames) ** (-0.5)

    at = section % 2 * 32 + x * 16 + z * 4 + y
    table = lax.dynamic_index_in_dim(jnp.asarray(tables()), at, 0, keepdims=False)
    meta = jnp.concatenate([section[None], lens, x[None], jnp.zeros((4,), jnp.int32), table])

    place = (x * 16 + z * 4 + y) * 48
    small = jnp.pad(jnp.concatenate([depth_kernel[0], norm_gain[0:1]], axis=0), ((0, 2), (0, 0)))
    small = lax.dynamic_update_slice(jnp.zeros((8, features), BF16), small, (0, place))
    weights, small = gather_weights(pointwise[0], small)
    taps = small.astype(F32)
    made = [forward(0, lens, inputs, taps)] * 2

    def turn(state, come, come_one, who):
        saved = [made[m][i] for i in range(3) for m in range(2)]
        return relay(who, meta, grads, come, come_one, weights, saved, taps, state)

    def hop(block, source):
        return lax.ppermute(block, "section", [(source, source - 1)])

    outs = [None] * 6
    outs[0], state = turn(None, made[0][0], made[0][0], (-1, -1, -1, 0))
    two_0 = hop(outs[0], 3)
    later, _ = lax.optimization_barrier((taps, outs[0]))
    made[1] = forward(1, lens, inputs, later)
    acts = [made[0][3], made[1][3]]
    outs[1], state = turn(state, two_0, two_0, (-1, -1, 0, 1))
    two_1, one_0 = hop(outs[1], 3), hop(outs[1], 2)
    outs[2], state = turn(state, two_1, two_1, (-1, -1, 1, -1))
    one_1 = hop(outs[2], 2)
    outs[3], state = turn(state, one_0, one_0, (-1, 0, -1, -1))
    outs[3], one_1 = lax.optimization_barrier((outs[3], one_1))
    zero_0 = hop(outs[3], 1)
    outs[4], state = turn(state, zero_0, one_1, (0, 1, -1, -1))
    zero_1 = hop(outs[4], 1)
    sums_0, _ = tap_terms(0, meta, inputs, *state, taps, outs[:0])
    zero_1, sums_0 = lax.optimization_barrier((zero_1, sums_0))
    parts = weight_terms(meta, acts, grads, [zero_0, zero_1, one_0, one_1, two_0, two_1])
    outs[5], state = turn(state, zero_1, zero_1, (1, -1, -1, -1))
    sums_1, frame_out = tap_terms(1, meta, inputs, *state, taps, outs)
    sums = sums_0 + sums_1

    point_share, sums = scatter_weights(parts, sums * factor)
    share = lax.dynamic_slice(sums, (0, place), (8, 48))
    return (
        frame_out[None, :, None],
        (point_share * factor)[None],
        share[None, :5],
        share[5:6],
    )


def solution(mesh):
    fine = Mesh(mesh.devices.reshape(4, 2, 4, 4), ("section", "xh", "z", "y"))
    fsdp = ("xh", "z", "y")
    return jax.shard_map(
        body,
        mesh=fine,
        in_specs=(
            P("section", None, fsdp, None, None),
            P(None, fsdp, None, None),
            P(None, fsdp),
            P("section", fsdp, None),
            P("section", None, fsdp),
            P("section", fsdp),
        ),
        out_specs=(
            P("section", None, fsdp, None, None),
            P("section", fsdp, None),
            P("section", None, fsdp),
            P("section", fsdp),
        ),
        check_vma=False,
    )
```

```python
import functools

import jax
import jax.numpy as jnp
import numpy as np
from jax import lax
from jax.experimental import pallas as pl
from jax.experimental.pallas import tpu as pltpu
from jax.sharding import Mesh
from jax.sharding import PartitionSpec as P

EPSILON = 1e-05
F32 = jnp.float32
BF16 = jnp.bfloat16
LANES = 128
PAD = 8
ANY = pl.BlockSpec(memory_space=pl.ANY)
HBM = pl.BlockSpec(memory_space=pltpu.HBM)
SMEM = pl.BlockSpec(memory_space=pltpu.SMEM)
VMEM = pl.BlockSpec(memory_space=pltpu.VMEM)

def params(limit, **kw):
    return pltpu.CompilerParams(vmem_limit_bytes=limit << 20, **kw)


def cost(us):
    return pl.CostEstimate(flops=int(us * 1.0e9), bytes_accessed=1 << 20, transcendentals=0)


def partners(core):
    near, mirrored = [i ^ 1 for i in range(4)], [3 - i for i in range(4)]
    return (near, mirrored) if core == 0 else (mirrored, near)


def tables():
    gather = np.zeros((2, 2, 4, 4, 2, 4, 4, 2), np.int32)
    scatter = np.zeros((2, 2, 4, 4, 2, 32), np.int32)
    for core, x, z, y, half in np.ndindex(2, 2, 4, 4, 2):
        inner, outer = (y, z) if half == 0 else (z, y)
        one, two = partners(core)

        def block(a, b, r):
            zz, yy = (a, b) if half == 0 else (b, a)
            return (x + r) % 2 * 16 + zz * 4 + yy

        def order(me):
            return me, one[me], two[me], one[two[me]]

        for o, a in enumerate(order(outer)):
            for i, b in enumerate(order(inner)):
                for r in range(2):
                    gather[core, x, z, y, half, o, i, r] = block(a, b, r)
                    at = (3, 1, 2, 0)
                    place = at.index(o) * 8 + at.index(i) * 2 + r
                    scatter[core, x, z, y, half, block(a, b, r)] = place
    return np.concatenate([gather.reshape(64, -1), scatter.reshape(64, -1)], axis=-1)


def forward_kernel(m, lens, x_in, taps, normed_out, slope_out, inv_out, act_out, *rest):
    x_ref, hid, mix, normed_ref, slope_ref, inv_ref, act, act_ref, low, sem, sems = rest
    length = lens[m]
    frames, feats = x_ref.shape
    cols = feats // LANES
    copy = pltpu.make_async_copy(x_in.at[m], x_ref, sem)
    copy.start()
    for c in range(cols):
        hid[c, 0:PAD, :] = jnp.zeros((PAD, LANES), F32)
        hid[c, PAD + frames : 2 * PAD + frames, :] = jnp.zeros((PAD, LANES), F32)
    copy.wait()

    def load(i, carry):
        r = pl.multiple_of(i * 16, 16)
        rows = r + lax.broadcasted_iota(jnp.int32, (16, LANES), 0)
        keep = rows < length
        for c in range(cols):
            v = x_ref[pl.ds(r, 16), c * LANES : (c + 1) * LANES].astype(F32)
            hid[c, pl.ds(r + PAD, 16), :] = jnp.where(keep, v, 0.0)
        return carry

    lax.fori_loop(0, frames // 16, load, 0, unroll=2)

    def conv(i, carry):
        r = pl.multiple_of(i * 64, 64)
        whole = jnp.zeros((64, LANES), F32)
        for c in range(cols):
            span = slice(c * LANES, (c + 1) * LANES)
            total = taps[0:1, span] * hid[c, pl.ds(r + PAD - 2, 64), :]
            for k in range(1, 5):
                total = total + taps[k : k + 1, span] * hid[c, pl.ds(r + PAD - 2 + k, 64), :]
            mix[pl.ds(r, 64), span] = total
            whole = whole + total
        mean = jnp.sum(whole, axis=-1, keepdims=True) * (1.0 / feats)
        low[pl.ds(r, 64), :] = jnp.broadcast_to(mean, (64, LANES))
        return carry

    lax.fori_loop(0, frames // 64, conv, 0)

    def centre(i, carry):
        r = pl.multiple_of(i * 64, 64)
        mean = low[pl.ds(r, 64), :]
        whole = jnp.zeros((64, LANES), F32)
        for c in range(cols):
            span = slice(c * LANES, (c + 1) * LANES)
            centred = mix[pl.ds(r, 64), span] - mean
            mix[pl.ds(r, 64), span] = centred
            whole = whole + centred * centred
        spread = jnp.sum(whole, axis=-1, keepdims=True) * (1.0 / feats)
        inv_ref[pl.ds(r, 64), :] = jnp.broadcast_to(lax.rsqrt(spread + EPSILON), (64, LANES))
        return carry

    lax.fori_loop(0, frames // 64, centre, 0, unroll=2)

    def norm(i, carry):
        r = pl.multiple_of(i * 16, 16)
        keep = r + lax.broadcasted_iota(jnp.int32, (16, LANES), 0) < length
        inverse = inv_ref[pl.ds(r, 16), :]
        for c in range(cols):
            span = slice(c * LANES, (c + 1) * LANES)
            gain = taps[5:6, span]
            normed = mix[pl.ds(r, 16), span] * inverse
            gained = normed * gain
            logistic = jax.nn.sigmoid(gained)
            normed_ref[pl.ds(r, 16), span] = normed.astype(BF16)
            slope = (logistic + gained * logistic * (1.0 - logistic)) * gain
            slope_ref[pl.ds(r, 16), span] = jnp.where(keep, slope, 0.0).astype(BF16)
            act[pl.ds(r, 16), span] = jnp.where(keep, gained * logistic, 0.0).astype(BF16)
        return carry

    outs = ((normed_ref, normed_out), (slope_ref, slope_out), (inv_ref, inv_out))

    def quarter(q, carry):
        lax.fori_loop(0, frames // 64, lambda i, c: norm(q * (frames // 64) + i, c), 0, unroll=2)
        part = pl.ds(pl.multiple_of(q * (frames // 4), frames // 4), frames // 4)
        for n, (held, out) in enumerate(outs):
            pltpu.make_async_copy(held.at[part], out.at[part], sems.at[n]).start()
        return carry

    lax.fori_loop(0, 4, quarter, 0)
    for c in range(feats // 256):
        span = slice(c * 256, (c + 1) * 256)
        act_ref[span, :] = act[:, span].T
        pltpu.make_async_copy(act_ref.at[span], act_out.at[span], sems.at[3]).start()
    for n, (held, out) in enumerate(outs + ((act_ref, act_out),)):
        pltpu.make_async_copy(held, out, sems.at[n]).wait()


def forward(m, lens, x, taps):
    micro, frames, feats = x.shape
    return pl.pallas_call(
        functools.partial(forward_kernel, m),
        in_specs=[SMEM, HBM, VMEM],
        out_specs=[HBM] * 4,
        out_shape=[
            jax.ShapeDtypeStruct((frames, feats), BF16),
            jax.ShapeDtypeStruct((frames, feats), BF16),
            jax.ShapeDtypeStruct((frames, LANES), F32),
            jax.ShapeDtypeStruct((feats, frames), BF16),
        ],
        scratch_shapes=[
            pltpu.VMEM((frames, feats), BF16),
            pltpu.VMEM((feats // LANES, frames + 2 * PAD, LANES), F32),
            pltpu.VMEM((frames, feats), F32),
            pltpu.VMEM((frames, feats), BF16),
            pltpu.VMEM((frames, feats), BF16),
            pltpu.VMEM((frames, LANES), F32),
            pltpu.VMEM((frames, feats), BF16),
            pltpu.VMEM((feats, frames), BF16),
            pltpu.VMEM((frames, LANES), F32),
            pltpu.SemaphoreType.DMA,
            pltpu.SemaphoreType.DMA((4,)),
        ],
        compiler_params=params(60),
        cost_estimate=cost(8),
    )(lens, x, taps)


def relay_kernel(first, who, meta, grads, come, come_one, *rest):
    (wa, wb), rest = (rest[:2], rest[2:4]), rest[4:]
    (normed_in, slope_in, inv_in), taps, rest = (rest[0:2], rest[2:4], rest[4:6]), rest[6], rest[7:]
    if not first:
        rest = rest[2:]
    send, mixed_out, gain_out = rest[:3]
    w, up, normed, slope, inv, ga, gmix, narrow, out, gsum, low, high, sems = rest[3:]
    frames, feats = up.shape
    cols = feats // LANES
    half = feats // 2
    rows = 48
    section, place_x = meta[0], meta[3]
    turn = sum(jnp.where(section == i, m, 0) for i, m in enumerate(who))
    active, slot = turn >= 0, jnp.maximum(turn, 0)
    last, length = section == 3, meta[1 + slot]

    def pieces(group):
        made = []
        odd = (place_x + group) % 2
        for h, parts in enumerate((wa, wb)):
            for p in range(2):
                for j in range(8):
                    at = h * 32 + p * 16 + 2 * j + odd
                    place = pl.multiple_of(meta[8 + at] * rows, 16)
                    made.append(
                        pltpu.make_async_copy(
                            parts[p].at[2 * j + odd],
                            w.at[pl.ds(place, rows), pl.ds(h * half, half)],
                            sems.at[0 if group == 0 else 8],
                        )
                    )
        return made

    @pl.when(active)
    def _():
        @pl.when(last)
        def _():
            pltpu.make_async_copy(grads.at[slot], up, sems.at[1]).start()

        @pl.when(section == 1)
        def _():
            pltpu.make_async_copy(come_one, up, sems.at[1]).start()

        @pl.when(jnp.logical_and(section != 3, section != 1))
        def _():
            pltpu.make_async_copy(come, up, sems.at[1]).start()

        weights = [pieces(0), pieces(1)]
        for copy in weights[0]:
            copy.start()
        for m in range(2):

            @pl.when(slot == m)
            def _():
                pltpu.make_async_copy(slope_in[m], slope, sems.at[3]).start()
                pltpu.make_async_copy(normed_in[m], normed, sems.at[2]).start()
                pltpu.make_async_copy(inv_in[m], inv, sems.at[4]).start()

        for copy in weights[1]:
            copy.start()
        for c in range(cols):
            gmix[c, 0:PAD, :] = jnp.zeros((PAD, LANES), F32)
            gmix[c, PAD + frames : 2 * PAD + frames, :] = jnp.zeros((PAD, LANES), F32)
        low[...] = jnp.zeros_like(low)
        high[...] = jnp.zeros_like(high)

        def multiply(n):
            ga[:, n * 256 : (n + 1) * 256] = lax.dot_general(
                up[...],
                w[n * 256 : (n + 1) * 256, :],
                (((1,), (1,)), ((), ())),
                preferred_element_type=F32,
            )

        def weigh(n):
            span = slice(n * 256, (n + 1) * 256)
            total = jnp.zeros((8, 256), F32)
            for r in range(0, frames, 32):
                part = slice(r, r + 32)
                gn = ga[part, span] * slope[part, span].astype(F32)
                both = gn * normed[part, span].astype(F32)
                ga[part, span] = gn
                low[part, :] += gn[:, :LANES] + gn[:, LANES:]
                high[part, :] += both[:, :LANES] + both[:, LANES:]
                total = total + (both[:8] + both[8:16]) + (both[16:24] + both[24:])
            gsum[:, span] = total

        pltpu.make_async_copy(come, up, sems.at[1]).wait()
        for copy in weights[0]:
            copy.wait()
        multiply(0)
        pltpu.make_async_copy(slope_in[0], slope, sems.at[3]).wait()
        pltpu.make_async_copy(normed_in[0], normed, sems.at[2]).wait()
        pltpu.make_async_copy(inv_in[0], inv, sems.at[4]).wait()
        count = feats // 256
        for n in range(1, count):
            if n == count // 2:
                for copy in weights[1]:
                    copy.wait()
            multiply(n)
            weigh(n - 1)
        weigh(count - 1)
        gain_copy = pltpu.make_async_copy(gsum, gain_out.at[slot], sems.at[6])
        gain_copy.start()

        def means(i, carry):
            r = pl.multiple_of(i * 64, 64)
            for ref in (low, high):
                mean = jnp.sum(ref[pl.ds(r, 64), :], axis=-1, keepdims=True) * (1.0 / feats)
                ref[pl.ds(r, 64), :] = jnp.broadcast_to(mean, (64, LANES))
            return carry

        lax.fori_loop(0, frames // 64, means, 0, unroll=2)

        def finish(i, carry):
            r = pl.multiple_of(i * 16, 16)
            a, b, scale = low[pl.ds(r, 16), :], high[pl.ds(r, 16), :], inv[pl.ds(r, 16), :]
            for c in range(cols):
                span = slice(c * LANES, (c + 1) * LANES)
                nm = normed[pl.ds(r, 16), span].astype(F32)
                mixed = scale * (ga[pl.ds(r, 16), span] - a - nm * b)
                narrow[pl.ds(r, 16), span] = mixed.astype(BF16)
                gmix[c, pl.ds(r + PAD, 16), :] = mixed
            return carry

        lax.fori_loop(0, frames // 16, finish, 0, unroll=2)
        saved = pltpu.make_async_copy(narrow, mixed_out.at[slot], sems.at[5])
        saved.start()

        def conv(i, carry):
            r = pl.multiple_of(i * 64, 64)
            keep = r + lax.broadcasted_iota(jnp.int32, (64, LANES), 0) < length
            for c in range(cols):
                span = slice(c * LANES, (c + 1) * LANES)
                total = taps[4:5, span] * gmix[c, pl.ds(r + PAD - 2, 64), :]
                for k in range(1, 5):
                    total = total + taps[4 - k : 5 - k, span] * gmix[c, pl.ds(r + PAD - 2 + k, 64), :]
                result = up[pl.ds(r, 64), span].astype(F32) + jnp.where(keep, total, 0.0)
                out[pl.ds(r, 64), span] = result.astype(BF16)
            part = pl.ds(r, 64)
            pltpu.make_async_copy(out.at[part], send.at[part], sems.at[7]).start()
            return carry

        lax.fori_loop(0, frames // 64, conv, 0)
        pltpu.make_async_copy(out, send, sems.at[7]).wait()
        saved.wait()
        gain_copy.wait()


def relay(who, meta, grads, come, come_one, weights, saved, taps, state):
    micro, frames, feats = grads.shape
    cols = feats // LANES
    first = state is None
    shapes = [
        jax.ShapeDtypeStruct((frames, feats), BF16),
        jax.ShapeDtypeStruct((micro, frames, feats), BF16),
        jax.ShapeDtypeStruct((micro, 8, feats), F32),
    ]
    operands = [meta, grads, come, come_one, *weights, *saved, taps]
    specs = [SMEM, HBM, ANY, ANY] + [HBM] * (len(operands) - 5) + [VMEM]
    aliases = {}
    if not first:
        aliases = {len(operands) + i: 1 + i for i in range(2)}
        operands += list(state)
        specs += [HBM] * 2
    out = pl.pallas_call(
        functools.partial(relay_kernel, first, who),
        in_specs=specs,
        out_specs=[ANY] + [HBM] * 2,
        out_shape=shapes,
        input_output_aliases=aliases,
        scratch_shapes=[
            pltpu.VMEM((feats, feats), BF16),
            pltpu.VMEM((frames, feats), BF16),
            pltpu.VMEM((frames, feats), BF16),
            pltpu.VMEM((frames, feats), BF16),
            pltpu.VMEM((frames, LANES), F32),
            pltpu.VMEM((frames, feats), F32),
            pltpu.VMEM((cols, frames + 2 * PAD, LANES), F32),
            pltpu.VMEM((frames, feats), BF16),
            pltpu.VMEM((frames, feats), BF16),
            pltpu.VMEM((8, feats), F32),
            pltpu.VMEM((frames, LANES), F32),
            pltpu.VMEM((frames, LANES), F32),
            pltpu.SemaphoreType.DMA((10,)),
        ],
        compiler_params=params(60),
        cost_estimate=cost(1),
    )(*operands)
    return out[0], tuple(out[1:])


def weight_kernel(meta, act_a, act_b, *rest):
    sources, outs, (act, gm, acc, block, sems) = rest[:7], rest[7:11], rest[11:]
    feats, frames = act_a.shape
    half = feats // 2
    section = meta[0]
    copies = [
        pltpu.make_async_copy(act_a, act.at[:, pl.ds(0, frames)], sems.at[0]),
        pltpu.make_async_copy(act_b, act.at[:, pl.ds(frames, frames)], sems.at[1]),
    ]
    for copy in copies:
        copy.start()
    for m in range(2):
        for owner in range(4):

            @pl.when(section == owner)
            def _():
                source = sources[0].at[m] if owner == 3 else sources[1 + 2 * owner + m]
                place = gm.at[pl.ds(m * frames, frames)]
                pltpu.make_async_copy(source, place, sems.at[2 + m]).start()

    for m in range(2):
        copies[m].wait()
        pltpu.make_async_copy(sources[1], gm.at[pl.ds(m * frames, frames)], sems.at[2 + m]).wait()
    leaving = []
    rows = 48
    for h in range(2):

        def multiply(n, carry):
            r = pl.multiple_of(n * 384, 384)
            acc[...] = lax.dot_general(
                act[pl.ds(r, 384), :],
                gm[:, h * half : (h + 1) * half],
                (((1,), (0,)), ((), ())),
                preferred_element_type=F32,
            )
            for q in range(8):
                place = meta[72 + h * 32 + n * 8 + q]
                block[h, place] = acc[q * rows : (q + 1) * rows, :].astype(BF16)
            return carry

        lax.fori_loop(0, feats // 384, multiply, 0)
        for p in range(2):
            copy = pltpu.make_async_copy(
                block.at[h, pl.ds(p * 16, 16)], outs[h * 2 + p], sems.at[4 + h * 2 + p]
            )
            copy.start()
            leaving.append(copy)
    for copy in leaving:
        copy.wait()


def weight_terms(meta, acts, grads, comes):
    feats, frames = acts[0].shape
    half = feats // 2
    operands = [meta, *acts, grads, *comes]
    return pl.pallas_call(
        weight_kernel,
        in_specs=[SMEM, ANY, ANY, HBM] + [ANY] * len(comes),
        out_specs=[ANY] * 4,
        out_shape=[jax.ShapeDtypeStruct((16, 48, half), BF16)] * 4,
        scratch_shapes=[
            pltpu.VMEM((feats, 2 * frames), BF16),
            pltpu.VMEM((2 * frames, feats), BF16),
            pltpu.VMEM((384, half), F32),
            pltpu.VMEM((2, 32, 48, half), BF16),
            pltpu.SemaphoreType.DMA((12,)),
        ],
        compiler_params=params(60),
        cost_estimate=cost(8),
    )(*operands)


def tap_kernel(m, meta, x_in, mixed_in, gain_in, taps, *rest):
    count = 6 if m == 1 else 0
    sent, rest = rest[:count], rest[count:]
    if count:
        out, frame_out, x_ref, mixed_ref, gain_ref, hid, sems, held, more = rest
    else:
        out, x_ref, mixed_ref, gain_ref, hid, sems = rest
    section = meta[0]
    length = meta[1 + m]
    frames, feats = x_ref.shape
    cols = feats // LANES
    copies = [
        pltpu.make_async_copy(x_in.at[m], x_ref, sems.at[0]),
        pltpu.make_async_copy(mixed_in.at[m], mixed_ref, sems.at[1]),
        pltpu.make_async_copy(gain_in.at[m], gain_ref, sems.at[2]),
    ]
    for copy in copies:
        copy.start()
    if count:
        for owner, turns in enumerate(((4, 5), (3, 4), (1, 2), (0, 1))):

            @pl.when(section == owner)
            def _():
                for p in range(2):
                    pltpu.make_async_copy(sent[turns[p]], held.at[p], more.at[p]).start()

    for c in range(cols):
        hid[c, 0:PAD, :] = jnp.zeros((PAD, LANES), F32)
        hid[c, PAD + frames : 2 * PAD + frames, :] = jnp.zeros((PAD, LANES), F32)
    copies[0].wait()

    def load(i, carry):
        r = pl.multiple_of(i * 16, 16)
        keep = r + lax.broadcasted_iota(jnp.int32, (16, LANES), 0) < length
        for c in range(cols):
            v = x_ref[pl.ds(r, 16), c * LANES : (c + 1) * LANES].astype(F32)
            hid[c, pl.ds(r + PAD, 16), :] = jnp.where(keep, v, 0.0)
        return carry

    lax.fori_loop(0, frames // 16, load, 0, unroll=2)
    copies[1].wait()
    copies[2].wait()
    leave = None
    if count:
        for p in range(2):
            pltpu.make_async_copy(sent[0], held.at[p], more.at[p]).wait()
        leave = pltpu.make_async_copy(held, frame_out, more.at[2])
        leave.start()
    for c in range(cols):
        span = slice(c * LANES, (c + 1) * LANES)

        def add(i, sums):
            r = pl.multiple_of(i * 32, 32)
            grown = list(sums)
            wide = mixed_ref[pl.ds(r, 32), span].astype(F32)
            for q in range(4):
                g = wide[8 * q : 8 * q + 8]
                for k in range(5):
                    grown[k] = grown[k] + g * hid[c, pl.ds(r + PAD - 2 + k + 8 * q, 8), :]
            return tuple(grown)

        sums = lax.fori_loop(0, frames // 32, add, (jnp.zeros((8, LANES), F32),) * 5, unroll=2)
        for k in range(5):
            out[k : k + 1, span] = jnp.sum(sums[k], axis=0, keepdims=True)
    out[5:6, :] = jnp.sum(gain_ref[...], axis=0, keepdims=True) / taps[5:6, :]
    out[6:8, :] = jnp.zeros((2, feats), F32)
    if count:
        leave.wait()


def tap_terms(m, meta, x, mixed, gain, taps, sent):
    micro, frames, feats = x.shape
    more = len(sent) > 0
    made = pl.pallas_call(
        functools.partial(tap_kernel, m),
        in_specs=[SMEM, HBM, HBM, HBM, VMEM] + [HBM] * len(sent),
        out_specs=[VMEM] + [HBM] * more,
        out_shape=[jax.ShapeDtypeStruct((8, feats), F32)]
        + [jax.ShapeDtypeStruct(x.shape, BF16)] * more,
        scratch_shapes=[
            pltpu.VMEM((frames, feats), BF16),
            pltpu.VMEM((frames, feats), BF16),
            pltpu.VMEM((8, feats), F32),
            pltpu.VMEM((feats // LANES, frames + 2 * PAD, LANES), F32),
            pltpu.SemaphoreType.DMA((3,)),
        ]
        + [pltpu.VMEM(x.shape, BF16), pltpu.SemaphoreType.DMA((3,))] * more,
        compiler_params=params(60),
        cost_estimate=cost(5),
    )(meta, x, mixed, gain, taps, *sent)
    return made[0], (made[1] if more else None)


def early(x):
    return pl.pallas_call(
        lambda x_ref, out_ref: None,
        in_specs=[ANY],
        out_specs=ANY,
        out_shape=jax.ShapeDtypeStruct(x.shape, x.dtype),
        input_output_aliases={0: 0},
        compiler_params=params(60),
        cost_estimate=cost(30),
    )(x)


def swap(x, axis, d):
    n = lax.axis_size(axis)
    return lax.ppermute(x, axis, [(i, i ^ d) for i in range(n)])


def meet(x, axis, step):
    n = lax.axis_size(axis)
    route = [
        (s * n + i, s * n + partners(s % 2)[step][i])
        for s in range(lax.axis_size("section"))
        for i in range(n)
    ]
    return lax.ppermute(x, ("section", axis), route)


def gather_weights(shard, small, run):
    rows, width = shard.shape
    half = width // 2
    extra = jnp.concatenate([small[:, :half], small[:, half:]])
    own = [jnp.concatenate([shard[:, :half], extra]), shard[:, half:]]
    axes = ("y", "z")
    pieces = [jnp.stack([p, swap(p, "xh", 1)]) for p in own]
    for step in range(2):
        pieces = [jnp.concatenate([p, meet(p, a, step)]) for p, a in zip(pieces, axes)]
    small = jnp.sum(pieces[0][:, rows:].astype(F32), axis=0).astype(BF16)
    for step in range(2):
        small = small + meet(small, "z", step)
    pieces = [p[:, :rows] for p in pieces]
    small, pieces = lax.optimization_barrier((small, pieces))
    come = [meet(p, a, 0) for p, a in zip(pieces, axes[::-1])]
    whole = jnp.concatenate([small[:8], small[8:]], axis=1).astype(F32)
    made = [run(0, whole)]
    made, come, whole = lax.optimization_barrier((made, come, whole))
    pieces = [jnp.concatenate([p, c]) for p, c in zip(pieces, come)]
    pieces = [(p, meet(p, a, 1)) for p, a in zip(pieces, axes[::-1])]
    made.append(run(1, whole))
    return [*pieces[0], *pieces[1]], whole, made


def scatter_weights(parts, sums):
    axes = ("z", "y")
    sent, kept = parts[0::2], parts[1::2]
    moved = [meet(p, a, 0) for p, a in zip(sent, axes)]
    moved, sums = lax.optimization_barrier((moved, sums))
    half = sums.shape[1] // 2
    sums = jnp.concatenate([sums[:, :half], sums[:, half:]])
    grown = [k.astype(F32) + m.astype(F32) for k, m in zip(kept, moved)]
    onward = [g[:8].astype(BF16) for g in grown]
    onward, sums = lax.optimization_barrier((onward, sums))
    come = [meet(o, a, 1) for o, a in zip(onward, axes)]
    for step in range(2):
        sums = sums + meet(sums, "z", step)
    sums, come = lax.optimization_barrier((sums, come))
    blocks = [g[8:] + c.astype(F32) for g, c in zip(grown, come)]
    blocks[0] = jnp.concatenate([blocks[0], jnp.broadcast_to(sums, (8,) + sums.shape)], axis=1)
    own = []
    for b, axis in zip(blocks, axes[::-1]):
        b = b[4:] + meet(b[:4].astype(BF16), axis, 0).astype(F32)
        b = b[2:] + meet(b[:2].astype(BF16), axis, 1).astype(F32)
        own.append(b[0] + swap(b[1].astype(BF16), "xh", 1).astype(F32))
    rows = own[1].shape[0]
    sums = own[0][rows:]
    sums = jnp.concatenate([sums[:8], sums[8:]], axis=1)
    return jnp.concatenate([own[0][:rows], own[1]], axis=1), sums


def body(saved_inputs, grad_outputs, lengths, pointwise, depth_kernel, norm_gain):
    section = lax.axis_index("section")
    x, z, y = (lax.axis_index(a) for a in ("xh", "z", "y"))
    inputs = saved_inputs[0, :, 0]
    grads = grad_outputs[:, 0]
    lens = lengths[:, 0]
    micro, frames, features = inputs.shape
    factor = float(32 * micro * frames) ** (-0.5)

    at = section % 2 * 32 + x * 16 + z * 4 + y
    table = lax.dynamic_index_in_dim(jnp.asarray(tables()), at, 0, keepdims=False)
    meta = jnp.concatenate([section[None], lens, x[None], jnp.zeros((4,), jnp.int32), table])

    place = (x * 16 + z * 4 + y) * 48
    small = jnp.pad(jnp.concatenate([depth_kernel[0], norm_gain[0:1]], axis=0), ((0, 2), (0, 0)))
    small = lax.dynamic_update_slice(jnp.zeros((8, features), BF16), small, (0, place))

    weights, taps, made = gather_weights(
        pointwise[0], small, lambda m, taps: forward(m, lens, inputs, taps)
    )

    def turn(state, come, come_one, who):
        saved = [made[m][i] for i in range(3) for m in range(2)]
        return relay(who, meta, grads, come, come_one, weights, saved, taps, state)

    def hop(block, source):
        return lax.ppermute(block, "section", [(source, source - 1)])

    outs = [None] * 6
    outs[0], state = turn(None, made[0][0], made[0][0], (-1, -1, -1, 0))
    two_0 = hop(outs[0], 3)
    acts = [made[0][3], made[1][3]]
    outs[1], state = turn(state, two_0, two_0, (-1, -1, 0, 1))
    two_1, one_0 = hop(outs[1], 3), hop(outs[1], 2)
    outs[2], state = turn(state, two_1, two_1, (-1, -1, 1, -1))
    one_1 = hop(outs[2], 2)
    outs[3], state = turn(state, one_0, one_0, (-1, 0, -1, -1))
    zero_0 = hop(outs[3], 1)
    one_1 = early(one_1)
    outs[4], state = turn(state, zero_0, one_1, (0, 1, -1, -1))
    zero_1 = hop(outs[4], 1)
    sums_0, _ = tap_terms(0, meta, inputs, *state, taps, outs[:0])
    zero_1, sums_0 = lax.optimization_barrier((zero_1, sums_0))
    parts = weight_terms(meta, acts, grads, [zero_0, zero_1, one_0, one_1, two_0, two_1])
    outs[5], state = turn(state, zero_1, zero_1, (1, -1, -1, -1))
    sums_1, frame_out = tap_terms(1, meta, inputs, *state, taps, outs)
    sums = sums_0 + sums_1

    point_share, sums = scatter_weights(parts, sums * factor)
    share = lax.dynamic_slice(sums, (0, place), (8, 48))
    return (
        frame_out[None, :, None],
        (point_share * factor)[None],
        share[None, :5],
        share[5:6],
    )


def solution(mesh):
    fine = Mesh(mesh.devices.reshape(4, 2, 4, 4), ("section", "xh", "z", "y"))
    fsdp = ("xh", "z", "y")
    return jax.shard_map(
        body,
        mesh=fine,
        in_specs=(
            P("section", None, fsdp, None, None),
            P(None, fsdp, None, None),
            P(None, fsdp),
            P("section", fsdp, None),
            P("section", None, fsdp),
            P("section", fsdp),
        ),
        out_specs=(
            P("section", None, fsdp, None, None),
            P("section", fsdp, None),
            P("section", None, fsdp),
            P("section", fsdp),
        ),
        check_vma=False,
    )
```

```python
import functools

import jax
import jax.numpy as jnp
import numpy as np
from jax import lax
from jax.experimental import pallas as pl
from jax.experimental.pallas import tpu as pltpu
from jax.sharding import Mesh
from jax.sharding import PartitionSpec as P

EPSILON = 1e-05
F32 = jnp.float32
BF16 = jnp.bfloat16
LANES = 128
PAD = 8
ANY = pl.BlockSpec(memory_space=pl.ANY)
HBM = pl.BlockSpec(memory_space=pltpu.HBM)
SMEM = pl.BlockSpec(memory_space=pltpu.SMEM)
VMEM = pl.BlockSpec(memory_space=pltpu.VMEM)

def params(limit, **kw):
    return pltpu.CompilerParams(vmem_limit_bytes=limit << 20, **kw)


def cost(us):
    return pl.CostEstimate(flops=int(us * 1.0e9), bytes_accessed=1 << 20, transcendentals=0)


def partners(core):
    near, mirrored = [i ^ 1 for i in range(4)], [3 - i for i in range(4)]
    return (near, mirrored) if core == 0 else (mirrored, near)


def tables():
    gather = np.zeros((2, 2, 4, 4, 2, 4, 4, 2), np.int32)
    scatter = np.zeros((2, 2, 4, 4, 2, 32), np.int32)
    for core, x, z, y, half in np.ndindex(2, 2, 4, 4, 2):
        inner, outer = (y, z) if half == 0 else (z, y)
        one, two = partners(core)

        def block(a, b, r):
            zz, yy = (a, b) if half == 0 else (b, a)
            return (x + r) % 2 * 16 + zz * 4 + yy

        def order(me):
            return me, one[me], two[me], one[two[me]]

        for o, a in enumerate(order(outer)):
            for i, b in enumerate(order(inner)):
                for r in range(2):
                    gather[core, x, z, y, half, o, i, r] = block(a, b, r)
                    at = (3, 1, 2, 0)
                    place = at.index(o) * 8 + at.index(i) * 2 + r
                    scatter[core, x, z, y, half, block(a, b, r)] = place
    return np.concatenate([gather.reshape(64, -1), scatter.reshape(64, -1)], axis=-1)


def forward_kernel(m, lens, x_in, taps, normed_out, slope_out, inv_out, act_out, *rest):
    x_ref, hid, mix, normed_ref, slope_ref, inv_ref, act, act_ref, low, sem, sems = rest
    length = lens[m]
    frames, feats = x_ref.shape
    cols = feats // LANES
    copy = pltpu.make_async_copy(x_in.at[m], x_ref, sem)
    copy.start()
    for c in range(cols):
        hid[c, 0:PAD, :] = jnp.zeros((PAD, LANES), F32)
        hid[c, PAD + frames : 2 * PAD + frames, :] = jnp.zeros((PAD, LANES), F32)
    copy.wait()

    def load(i, carry):
        r = pl.multiple_of(i * 16, 16)
        rows = r + lax.broadcasted_iota(jnp.int32, (16, LANES), 0)
        keep = rows < length
        for c in range(cols):
            v = x_ref[pl.ds(r, 16), c * LANES : (c + 1) * LANES].astype(F32)
            hid[c, pl.ds(r + PAD, 16), :] = jnp.where(keep, v, 0.0)
        return carry

    lax.fori_loop(0, frames // 16, load, 0, unroll=2)

    def conv(i, carry):
        r = pl.multiple_of(i * 64, 64)
        whole = jnp.zeros((64, LANES), F32)
        for c in range(cols):
            span = slice(c * LANES, (c + 1) * LANES)
            total = taps[0:1, span] * hid[c, pl.ds(r + PAD - 2, 64), :]
            for k in range(1, 5):
                total = total + taps[k : k + 1, span] * hid[c, pl.ds(r + PAD - 2 + k, 64), :]
            mix[pl.ds(r, 64), span] = total
            whole = whole + total
        mean = jnp.sum(whole, axis=-1, keepdims=True) * (1.0 / feats)
        low[pl.ds(r, 64), :] = jnp.broadcast_to(mean, (64, LANES))
        return carry

    lax.fori_loop(0, frames // 64, conv, 0)

    def centre(i, carry):
        r = pl.multiple_of(i * 64, 64)
        mean = low[pl.ds(r, 64), :]
        whole = jnp.zeros((64, LANES), F32)
        for c in range(cols):
            span = slice(c * LANES, (c + 1) * LANES)
            centred = mix[pl.ds(r, 64), span] - mean
            mix[pl.ds(r, 64), span] = centred
            whole = whole + centred * centred
        spread = jnp.sum(whole, axis=-1, keepdims=True) * (1.0 / feats)
        inv_ref[pl.ds(r, 64), :] = jnp.broadcast_to(lax.rsqrt(spread + EPSILON), (64, LANES))
        return carry

    lax.fori_loop(0, frames // 64, centre, 0, unroll=2)

    def norm(i, carry):
        r = pl.multiple_of(i * 16, 16)
        keep = r + lax.broadcasted_iota(jnp.int32, (16, LANES), 0) < length
        inverse = inv_ref[pl.ds(r, 16), :]
        for c in range(cols):
            span = slice(c * LANES, (c + 1) * LANES)
            gain = taps[5:6, span]
            normed = mix[pl.ds(r, 16), span] * inverse
            gained = normed * gain
            logistic = jax.nn.sigmoid(gained)
            normed_ref[pl.ds(r, 16), span] = normed.astype(BF16)
            slope = (logistic + gained * logistic * (1.0 - logistic)) * gain
            slope_ref[pl.ds(r, 16), span] = jnp.where(keep, slope, 0.0).astype(BF16)
            act[pl.ds(r, 16), span] = jnp.where(keep, gained * logistic, 0.0).astype(BF16)
        return carry

    outs = ((normed_ref, normed_out), (slope_ref, slope_out), (inv_ref, inv_out))

    def quarter(q, carry):
        lax.fori_loop(0, frames // 64, lambda i, c: norm(q * (frames // 64) + i, c), 0, unroll=2)
        part = pl.ds(pl.multiple_of(q * (frames // 4), frames // 4), frames // 4)
        for n, (held, out) in enumerate(outs):
            pltpu.make_async_copy(held.at[part], out.at[part], sems.at[n]).start()
        return carry

    lax.fori_loop(0, 4, quarter, 0)
    for c in range(feats // 256):
        span = slice(c * 256, (c + 1) * 256)
        act_ref[span, :] = act[:, span].T
        pltpu.make_async_copy(act_ref.at[span], act_out.at[span], sems.at[3]).start()
    for n, (held, out) in enumerate(outs + ((act_ref, act_out),)):
        pltpu.make_async_copy(held, out, sems.at[n]).wait()


def forward(m, lens, x, taps):
    micro, frames, feats = x.shape
    return pl.pallas_call(
        functools.partial(forward_kernel, m),
        in_specs=[SMEM, HBM, VMEM],
        out_specs=[HBM] * 4,
        out_shape=[
            jax.ShapeDtypeStruct((frames, feats), BF16),
            jax.ShapeDtypeStruct((frames, feats), BF16),
            jax.ShapeDtypeStruct((frames, LANES), F32),
            jax.ShapeDtypeStruct((feats, frames), BF16),
        ],
        scratch_shapes=[
            pltpu.VMEM((frames, feats), BF16),
            pltpu.VMEM((feats // LANES, frames + 2 * PAD, LANES), F32),
            pltpu.VMEM((frames, feats), F32),
            pltpu.VMEM((frames, feats), BF16),
            pltpu.VMEM((frames, feats), BF16),
            pltpu.VMEM((frames, LANES), F32),
            pltpu.VMEM((frames, feats), BF16),
            pltpu.VMEM((feats, frames), BF16),
            pltpu.VMEM((frames, LANES), F32),
            pltpu.SemaphoreType.DMA,
            pltpu.SemaphoreType.DMA((4,)),
        ],
        compiler_params=params(60),
        cost_estimate=cost(8),
    )(lens, x, taps)


def relay_kernel(first, who, meta, grads, come, come_one, *rest):
    (wa, wb), rest = (rest[:4], rest[4:8]), rest[8:]
    (normed_in, slope_in, inv_in), taps, rest = (rest[0:2], rest[2:4], rest[4:6]), rest[6], rest[7:]
    if not first:
        rest = rest[2:]
    send, mixed_out, gain_out = rest[:3]
    w, up, normed, slope, inv, ga, gmix, narrow, out, gsum, low, high, sems = rest[3:]
    frames, feats = up.shape
    cols = feats // LANES
    half = feats // 2
    rows = 48
    section, place_x = meta[0], meta[3]
    turn = sum(jnp.where(section == i, m, 0) for i, m in enumerate(who))
    active, slot = turn >= 0, jnp.maximum(turn, 0)
    last, length = section == 3, meta[1 + slot]

    def pieces(group):
        made = []
        odd = (place_x + group) % 2
        for h, parts in enumerate((wa, wb)):
            for p in range(4):
                for j in range(4):
                    at = h * 32 + p * 8 + 2 * j + odd
                    place = pl.multiple_of(meta[8 + at] * rows, 16)
                    made.append(
                        pltpu.make_async_copy(
                            parts[p].at[2 * j + odd],
                            w.at[pl.ds(place, rows), pl.ds(h * half, half)],
                            sems.at[0 if group == 0 else 8],
                        )
                    )
        return made

    @pl.when(active)
    def _():
        @pl.when(last)
        def _():
            pltpu.make_async_copy(grads.at[slot], up, sems.at[1]).start()

        @pl.when(section == 1)
        def _():
            pltpu.make_async_copy(come_one, up, sems.at[1]).start()

        @pl.when(jnp.logical_and(section != 3, section != 1))
        def _():
            pltpu.make_async_copy(come, up, sems.at[1]).start()

        weights = [pieces(0), pieces(1)]
        for copy in weights[0]:
            copy.start()
        for m in range(2):

            @pl.when(slot == m)
            def _():
                pltpu.make_async_copy(slope_in[m], slope, sems.at[3]).start()
                pltpu.make_async_copy(normed_in[m], normed, sems.at[2]).start()
                pltpu.make_async_copy(inv_in[m], inv, sems.at[4]).start()

        for copy in weights[1]:
            copy.start()
        for c in range(cols):
            gmix[c, 0:PAD, :] = jnp.zeros((PAD, LANES), F32)
            gmix[c, PAD + frames : 2 * PAD + frames, :] = jnp.zeros((PAD, LANES), F32)
        low[...] = jnp.zeros_like(low)
        high[...] = jnp.zeros_like(high)

        def multiply(n):
            ga[:, n * 256 : (n + 1) * 256] = lax.dot_general(
                up[...],
                w[n * 256 : (n + 1) * 256, :],
                (((1,), (1,)), ((), ())),
                preferred_element_type=F32,
            )

        def weigh(n):
            span = slice(n * 256, (n + 1) * 256)
            total = jnp.zeros((8, 256), F32)
            for r in range(0, frames, 32):
                part = slice(r, r + 32)
                gn = ga[part, span] * slope[part, span].astype(F32)
                both = gn * normed[part, span].astype(F32)
                ga[part, span] = gn
                low[part, :] += gn[:, :LANES] + gn[:, LANES:]
                high[part, :] += both[:, :LANES] + both[:, LANES:]
                total = total + (both[:8] + both[8:16]) + (both[16:24] + both[24:])
            gsum[:, span] = total

        pltpu.make_async_copy(come, up, sems.at[1]).wait()
        for copy in weights[0]:
            copy.wait()
        multiply(0)
        pltpu.make_async_copy(slope_in[0], slope, sems.at[3]).wait()
        pltpu.make_async_copy(normed_in[0], normed, sems.at[2]).wait()
        pltpu.make_async_copy(inv_in[0], inv, sems.at[4]).wait()
        count = feats // 256
        for n in range(1, count):
            if n == count // 2:
                for copy in weights[1]:
                    copy.wait()
            multiply(n)
            weigh(n - 1)
        weigh(count - 1)
        gain_copy = pltpu.make_async_copy(gsum, gain_out.at[slot], sems.at[6])
        gain_copy.start()

        def means(i, carry):
            r = pl.multiple_of(i * 64, 64)
            for ref in (low, high):
                mean = jnp.sum(ref[pl.ds(r, 64), :], axis=-1, keepdims=True) * (1.0 / feats)
                ref[pl.ds(r, 64), :] = jnp.broadcast_to(mean, (64, LANES))
            return carry

        lax.fori_loop(0, frames // 64, means, 0, unroll=2)

        def finish(i, carry):
            r = pl.multiple_of(i * 16, 16)
            a, b, scale = low[pl.ds(r, 16), :], high[pl.ds(r, 16), :], inv[pl.ds(r, 16), :]
            for c in range(cols):
                span = slice(c * LANES, (c + 1) * LANES)
                nm = normed[pl.ds(r, 16), span].astype(F32)
                mixed = scale * (ga[pl.ds(r, 16), span] - a - nm * b)
                narrow[pl.ds(r, 16), span] = mixed.astype(BF16)
                gmix[c, pl.ds(r + PAD, 16), :] = mixed
            return carry

        lax.fori_loop(0, frames // 16, finish, 0, unroll=2)
        saved = pltpu.make_async_copy(narrow, mixed_out.at[slot], sems.at[5])
        saved.start()

        def conv(i, carry):
            r = pl.multiple_of(i * 64, 64)
            keep = r + lax.broadcasted_iota(jnp.int32, (64, LANES), 0) < length
            for c in range(cols):
                span = slice(c * LANES, (c + 1) * LANES)
                total = taps[4:5, span] * gmix[c, pl.ds(r + PAD - 2, 64), :]
                for k in range(1, 5):
                    total = total + taps[4 - k : 5 - k, span] * gmix[c, pl.ds(r + PAD - 2 + k, 64), :]
                result = up[pl.ds(r, 64), span].astype(F32) + jnp.where(keep, total, 0.0)
                out[pl.ds(r, 64), span] = result.astype(BF16)
            part = pl.ds(r, 64)
            pltpu.make_async_copy(out.at[part], send.at[part], sems.at[7]).start()
            return carry

        lax.fori_loop(0, frames // 64, conv, 0)
        pltpu.make_async_copy(out, send, sems.at[7]).wait()
        saved.wait()
        gain_copy.wait()


def relay(who, meta, grads, come, come_one, weights, saved, taps, state):
    micro, frames, feats = grads.shape
    cols = feats // LANES
    first = state is None
    shapes = [
        jax.ShapeDtypeStruct((frames, feats), BF16),
        jax.ShapeDtypeStruct((micro, frames, feats), BF16),
        jax.ShapeDtypeStruct((micro, 8, feats), F32),
    ]
    operands = [meta, grads, come, come_one, *weights, *saved, taps]
    specs = [SMEM, HBM, ANY, ANY] + [HBM] * (len(operands) - 5) + [VMEM]
    aliases = {}
    if not first:
        aliases = {len(operands) + i: 1 + i for i in range(2)}
        operands += list(state)
        specs += [HBM] * 2
    out = pl.pallas_call(
        functools.partial(relay_kernel, first, who),
        in_specs=specs,
        out_specs=[ANY] + [HBM] * 2,
        out_shape=shapes,
        input_output_aliases=aliases,
        scratch_shapes=[
            pltpu.VMEM((feats, feats), BF16),
            pltpu.VMEM((frames, feats), BF16),
            pltpu.VMEM((frames, feats), BF16),
            pltpu.VMEM((frames, feats), BF16),
            pltpu.VMEM((frames, LANES), F32),
            pltpu.VMEM((frames, feats), F32),
            pltpu.VMEM((cols, frames + 2 * PAD, LANES), F32),
            pltpu.VMEM((frames, feats), BF16),
            pltpu.VMEM((frames, feats), BF16),
            pltpu.VMEM((8, feats), F32),
            pltpu.VMEM((frames, LANES), F32),
            pltpu.VMEM((frames, LANES), F32),
            pltpu.SemaphoreType.DMA((10,)),
        ],
        compiler_params=params(60),
        cost_estimate=cost(1),
    )(*operands)
    return out[0], tuple(out[1:])


def weight_kernel(meta, act_a, act_b, *rest):
    sources, outs, (act, gm, acc, block, sems) = rest[:7], rest[7:11], rest[11:]
    feats, frames = act_a.shape
    half = feats // 2
    section = meta[0]
    copies = [
        pltpu.make_async_copy(act_a, act.at[:, pl.ds(0, frames)], sems.at[0]),
        pltpu.make_async_copy(act_b, act.at[:, pl.ds(frames, frames)], sems.at[1]),
    ]
    for copy in copies:
        copy.start()
    for m in range(2):
        for owner in range(4):

            @pl.when(section == owner)
            def _():
                source = sources[0].at[m] if owner == 3 else sources[1 + 2 * owner + m]
                place = gm.at[pl.ds(m * frames, frames)]
                pltpu.make_async_copy(source, place, sems.at[2 + m]).start()

    for m in range(2):
        copies[m].wait()
        pltpu.make_async_copy(sources[1], gm.at[pl.ds(m * frames, frames)], sems.at[2 + m]).wait()
    leaving = []
    rows = 48
    for h in range(2):

        def multiply(n, carry):
            r = pl.multiple_of(n * 384, 384)
            acc[...] = lax.dot_general(
                act[pl.ds(r, 384), :],
                gm[:, h * half : (h + 1) * half],
                (((1,), (0,)), ((), ())),
                preferred_element_type=F32,
            )
            for q in range(8):
                place = meta[72 + h * 32 + n * 8 + q]
                block[h, place] = acc[q * rows : (q + 1) * rows, :].astype(BF16)
            return carry

        lax.fori_loop(0, feats // 384, multiply, 0)
        for p in range(2):
            copy = pltpu.make_async_copy(
                block.at[h, pl.ds(p * 16, 16)], outs[h * 2 + p], sems.at[4 + h * 2 + p]
            )
            copy.start()
            leaving.append(copy)
    for copy in leaving:
        copy.wait()


def weight_terms(meta, acts, grads, comes):
    feats, frames = acts[0].shape
    half = feats // 2
    operands = [meta, *acts, grads, *comes]
    return pl.pallas_call(
        weight_kernel,
        in_specs=[SMEM, ANY, ANY, HBM] + [ANY] * len(comes),
        out_specs=[ANY] * 4,
        out_shape=[jax.ShapeDtypeStruct((16, 48, half), BF16)] * 4,
        scratch_shapes=[
            pltpu.VMEM((feats, 2 * frames), BF16),
            pltpu.VMEM((2 * frames, feats), BF16),
            pltpu.VMEM((384, half), F32),
            pltpu.VMEM((2, 32, 48, half), BF16),
            pltpu.SemaphoreType.DMA((12,)),
        ],
        compiler_params=params(60),
        cost_estimate=cost(8),
    )(*operands)


def tap_kernel(m, meta, x_in, mixed_in, gain_in, taps, *rest):
    count = 6 if m == 1 else 0
    sent, rest = rest[:count], rest[count:]
    if count:
        out, frame_out, x_ref, mixed_ref, gain_ref, hid, sems, held, more = rest
    else:
        out, x_ref, mixed_ref, gain_ref, hid, sems = rest
    section = meta[0]
    length = meta[1 + m]
    frames, feats = x_ref.shape
    cols = feats // LANES
    copies = [
        pltpu.make_async_copy(x_in.at[m], x_ref, sems.at[0]),
        pltpu.make_async_copy(mixed_in.at[m], mixed_ref, sems.at[1]),
        pltpu.make_async_copy(gain_in.at[m], gain_ref, sems.at[2]),
    ]
    for copy in copies:
        copy.start()
    if count:
        for owner, turns in enumerate(((4, 5), (3, 4), (1, 2), (0, 1))):

            @pl.when(section == owner)
            def _():
                for p in range(2):
                    pltpu.make_async_copy(sent[turns[p]], held.at[p], more.at[p]).start()

    for c in range(cols):
        hid[c, 0:PAD, :] = jnp.zeros((PAD, LANES), F32)
        hid[c, PAD + frames : 2 * PAD + frames, :] = jnp.zeros((PAD, LANES), F32)
    copies[0].wait()

    def load(i, carry):
        r = pl.multiple_of(i * 16, 16)
        keep = r + lax.broadcasted_iota(jnp.int32, (16, LANES), 0) < length
        for c in range(cols):
            v = x_ref[pl.ds(r, 16), c * LANES : (c + 1) * LANES].astype(F32)
            hid[c, pl.ds(r + PAD, 16), :] = jnp.where(keep, v, 0.0)
        return carry

    lax.fori_loop(0, frames // 16, load, 0, unroll=2)
    copies[1].wait()
    copies[2].wait()
    leave = None
    if count:
        for p in range(2):
            pltpu.make_async_copy(sent[0], held.at[p], more.at[p]).wait()
        leave = pltpu.make_async_copy(held, frame_out, more.at[2])
        leave.start()
    for c in range(cols):
        span = slice(c * LANES, (c + 1) * LANES)

        def add(i, sums):
            r = pl.multiple_of(i * 32, 32)
            grown = list(sums)
            wide = mixed_ref[pl.ds(r, 32), span].astype(F32)
            for q in range(4):
                g = wide[8 * q : 8 * q + 8]
                for k in range(5):
                    grown[k] = grown[k] + g * hid[c, pl.ds(r + PAD - 2 + k + 8 * q, 8), :]
            return tuple(grown)

        sums = lax.fori_loop(0, frames // 32, add, (jnp.zeros((8, LANES), F32),) * 5, unroll=2)
        for k in range(5):
            out[k : k + 1, span] = jnp.sum(sums[k], axis=0, keepdims=True)
    out[5:6, :] = jnp.sum(gain_ref[...], axis=0, keepdims=True) / taps[5:6, :]
    out[6:8, :] = jnp.zeros((2, feats), F32)
    if count:
        leave.wait()


def tap_terms(m, meta, x, mixed, gain, taps, sent):
    micro, frames, feats = x.shape
    more = len(sent) > 0
    made = pl.pallas_call(
        functools.partial(tap_kernel, m),
        in_specs=[SMEM, HBM, HBM, HBM, VMEM] + [HBM] * len(sent),
        out_specs=[VMEM] + [HBM] * more,
        out_shape=[jax.ShapeDtypeStruct((8, feats), F32)]
        + [jax.ShapeDtypeStruct(x.shape, BF16)] * more,
        scratch_shapes=[
            pltpu.VMEM((frames, feats), BF16),
            pltpu.VMEM((frames, feats), BF16),
            pltpu.VMEM((8, feats), F32),
            pltpu.VMEM((feats // LANES, frames + 2 * PAD, LANES), F32),
            pltpu.SemaphoreType.DMA((3,)),
        ]
        + [pltpu.VMEM(x.shape, BF16), pltpu.SemaphoreType.DMA((3,))] * more,
        compiler_params=params(60),
        cost_estimate=cost(5),
    )(meta, x, mixed, gain, taps, *sent)
    return made[0], (made[1] if more else None)


def early(x):
    return pl.pallas_call(
        lambda x_ref, out_ref: None,
        in_specs=[ANY],
        out_specs=ANY,
        out_shape=jax.ShapeDtypeStruct(x.shape, x.dtype),
        input_output_aliases={0: 0},
        compiler_params=params(60),
        cost_estimate=cost(30),
    )(x)


def swap(x, axis, d):
    n = lax.axis_size(axis)
    return lax.ppermute(x, axis, [(i, i ^ d) for i in range(n)])


def meet(x, axis, step):
    n = lax.axis_size(axis)
    route = [
        (s * n + i, s * n + partners(s % 2)[step][i])
        for s in range(lax.axis_size("section"))
        for i in range(n)
    ]
    return lax.ppermute(x, ("section", axis), route)


def gather_weights(shard, small, run):
    rows, width = shard.shape
    half = width // 2
    extra = jnp.concatenate([small[:, :half], small[:, half:]])
    own = [jnp.concatenate([shard[:, :half], extra]), shard[:, half:]]
    axes = ("y", "z")
    pieces = [jnp.stack([p, swap(p, "xh", 1)]) for p in own]
    for step in range(2):
        pieces = [jnp.concatenate([p, meet(p, a, step)]) for p, a in zip(pieces, axes)]
    small = jnp.sum(pieces[0][:, rows:].astype(F32), axis=0).astype(BF16)
    for step in range(2):
        small = small + meet(small, "z", step)
    pieces = [p[:, :rows] for p in pieces]
    small, pieces = lax.optimization_barrier((small, pieces))
    come = [meet(p, a, 0) for p, a in zip(pieces, axes[::-1])]
    whole = jnp.concatenate([small[:8], small[8:]], axis=1).astype(F32)
    made = [run(0, whole)]
    far = [meet(p, a, 1) for p, a in zip(pieces, axes[::-1])]
    made, come, whole = lax.optimization_barrier((made, come, whole))
    pieces = [
        (p, c, f, meet(c, a, 1)) for p, c, f, a in zip(pieces, come, far, axes[::-1])
    ]
    made.append(run(1, whole))
    return [*pieces[0], *pieces[1]], whole, made


def scatter_weights(parts, sums):
    axes = ("z", "y")
    sent, kept = parts[0::2], parts[1::2]
    moved = [meet(p, a, 0) for p, a in zip(sent, axes)]
    moved, sums = lax.optimization_barrier((moved, sums))
    half = sums.shape[1] // 2
    sums = jnp.concatenate([sums[:, :half], sums[:, half:]])
    grown = [k.astype(F32) + m.astype(F32) for k, m in zip(kept, moved)]
    onward = [g[:8].astype(BF16) for g in grown]
    onward, sums = lax.optimization_barrier((onward, sums))
    come = [meet(o, a, 1) for o, a in zip(onward, axes)]
    for step in range(2):
        sums = sums + meet(sums, "z", step)
    sums, come = lax.optimization_barrier((sums, come))
    blocks = [g[8:] + c.astype(F32) for g, c in zip(grown, come)]
    blocks[0] = jnp.concatenate([blocks[0], jnp.broadcast_to(sums, (8,) + sums.shape)], axis=1)
    own = []
    for b, axis in zip(blocks, axes[::-1]):
        b = b[4:] + meet(b[:4].astype(BF16), axis, 0).astype(F32)
        b = b[2:] + meet(b[:2].astype(BF16), axis, 1).astype(F32)
        own.append(b[0] + swap(b[1].astype(BF16), "xh", 1).astype(F32))
    rows = own[1].shape[0]
    sums = own[0][rows:]
    sums = jnp.concatenate([sums[:8], sums[8:]], axis=1)
    return jnp.concatenate([own[0][:rows], own[1]], axis=1), sums


def body(saved_inputs, grad_outputs, lengths, pointwise, depth_kernel, norm_gain):
    section = lax.axis_index("section")
    x, z, y = (lax.axis_index(a) for a in ("xh", "z", "y"))
    inputs = saved_inputs[0, :, 0]
    grads = grad_outputs[:, 0]
    lens = lengths[:, 0]
    micro, frames, features = inputs.shape
    factor = float(32 * micro * frames) ** (-0.5)

    at = section % 2 * 32 + x * 16 + z * 4 + y
    table = lax.dynamic_index_in_dim(jnp.asarray(tables()), at, 0, keepdims=False)
    meta = jnp.concatenate([section[None], lens, x[None], jnp.zeros((4,), jnp.int32), table])

    place = (x * 16 + z * 4 + y) * 48
    small = jnp.pad(jnp.concatenate([depth_kernel[0], norm_gain[0:1]], axis=0), ((0, 2), (0, 0)))
    small = lax.dynamic_update_slice(jnp.zeros((8, features), BF16), small, (0, place))

    weights, taps, made = gather_weights(
        pointwise[0], small, lambda m, taps: forward(m, lens, inputs, taps)
    )

    def turn(state, come, come_one, who):
        saved = [made[m][i] for i in range(3) for m in range(2)]
        return relay(who, meta, grads, come, come_one, weights, saved, taps, state)

    def hop(block, source):
        return lax.ppermute(block, "section", [(source, source - 1)])

    outs = [None] * 6
    outs[0], state = turn(None, made[0][0], made[0][0], (-1, -1, -1, 0))
    two_0 = hop(outs[0], 3)
    acts = [made[0][3], made[1][3]]
    outs[1], state = turn(state, two_0, two_0, (-1, -1, 0, 1))
    two_1, one_0 = hop(outs[1], 3), hop(outs[1], 2)
    outs[2], state = turn(state, two_1, two_1, (-1, -1, 1, -1))
    one_1 = hop(outs[2], 2)
    outs[3], state = turn(state, one_0, one_0, (-1, 0, -1, -1))
    zero_0 = hop(outs[3], 1)
    one_1 = early(one_1)
    outs[4], state = turn(state, zero_0, one_1, (0, 1, -1, -1))
    zero_1 = hop(outs[4], 1)
    sums_0, _ = tap_terms(0, meta, inputs, *state, taps, outs[:0])
    zero_1, sums_0 = lax.optimization_barrier((zero_1, sums_0))
    parts = weight_terms(meta, acts, grads, [zero_0, zero_1, one_0, one_1, two_0, two_1])
    outs[5], state = turn(state, zero_1, zero_1, (1, -1, -1, -1))
    sums_1, frame_out = tap_terms(1, meta, inputs, *state, taps, outs)
    sums = sums_0 + sums_1

    point_share, sums = scatter_weights(parts, sums * factor)
    share = lax.dynamic_slice(sums, (0, place), (8, 48))
    return (
        frame_out[None, :, None],
        (point_share * factor)[None],
        share[None, :5],
        share[5:6],
    )


def solution(mesh):
    fine = Mesh(mesh.devices.reshape(4, 2, 4, 4), ("section", "xh", "z", "y"))
    fsdp = ("xh", "z", "y")
    return jax.shard_map(
        body,
        mesh=fine,
        in_specs=(
            P("section", None, fsdp, None, None),
            P(None, fsdp, None, None),
            P(None, fsdp),
            P("section", fsdp, None),
            P("section", None, fsdp),
            P("section", fsdp),
        ),
        out_specs=(
            P("section", None, fsdp, None, None),
            P("section", fsdp, None),
            P("section", None, fsdp),
            P("section", fsdp),
        ),
        check_vma=False,
    )
```
